512 devices in a mesh: probe: 32 (over z, core), seq: 16 (over x, y).
Axes of the slice: x: 4, y: 4, z: 16, core: 2. Of those that a mesh axis runs over, the one named last changes fastest.
Arguments:
- noisy: bfloat16 [512, 1152], P('seq'), may hold values from -6 to 6
- probes: bfloat16 [32, 512, 1152], P('probe', 'seq'), may hold values from -40 to 40
- w_qkv: bfloat16 [1152, 3456], P(None, 'seq'), may hold values from -0.1875 to 0.1875
- w_out: bfloat16 [1152, 1152], P('seq'), may hold values from -0.1875 to 0.1875
- w_mod: bfloat16 [256, 3456], replicated, may hold values from -0.375 to 0.375
- timestep: int32 [1], replicated, may hold values from 0 to 999
Outputs:
- basis: float32 [32, 512, 1152], P('probe', 'seq')
- factor: float32 [32, 32], replicated
The draws below stay inside these ranges and needn't reach their ends.
All inputs are finite; a program needn't handle non-finite values.
Results may differ from the reference program's by a relative error of at most 0.02.
Values may be sent and summed in bfloat16 or wider, within the bound.
No kernel may reach another device: no remote copies, remote signals or barrier semaphores. Data moves between devices by JAX's collectives and lax.ppermute only.
A program may use at most 64 MiB of HBM per device.

```python
import math
import jax
import jax.numpy as jnp
from jax import lax

HEADS = 16
HEAD_DIM = 72
FREQ_DIM = 256
D = 1152
FRAMES = 2
TOKENS = 512
FRAME_TOK = 256
PROBES = 32


def draw_probes(key, part):
    key = jax.random.fold_in(key, 7)
    key_base, key_rows, key_cols = jax.random.split(key, 3)
    row_scale = jnp.exp(jax.random.uniform(key_rows, (1, TOKENS, 1), jnp.float32, 0.0, math.log(10.0 / 3.0)))
    ramp = 3.0 ** (jnp.arange(TOKENS, dtype=jnp.float32) / max(TOKENS - 1, 1))
    col_scale = jnp.exp(jax.random.uniform(key_cols, (1, 1, D), jnp.float32, 0.0, math.log(10.0)))
    base_draw = jax.random.truncated_normal(key_base, -3.0, 3.0, (PROBES, TOKENS, D), jnp.float32)
    result = base_draw * row_scale * ramp.reshape(1, TOKENS, 1) * col_scale / 8.0
    return result.astype(jnp.bfloat16)


def levels(key, shape, pieces, least, largest):
    factor_of = 1.0
    for axis_at, shards_of in pieces:
        heights = jax.random.uniform(jax.random.fold_in(jax.random.fold_in(key, 6), axis_at), (shards_of,), jnp.float32, least / len(pieces), largest / len(pieces))
        factor_of = factor_of * jnp.repeat(jnp.exp(heights), shape[axis_at] // shards_of).reshape((-1,) + (1,) * (len(shape) - 1 - axis_at))
    return factor_of


def noise(own_key, dims, scale, limit, pieces=(), held_as=jnp.bfloat16):
    entries = jax.random.normal(own_key, dims, jnp.float32) * scale
    if len(pieces) > 0:
        entries = levels(own_key, dims, pieces, -0.22, 0.18) * entries
    return jnp.clip(entries, min=-limit, max=limit).astype(held_as)


def setup_inputs(seed: int = 0) -> dict:
    key_list = jax.random.split(jax.random.key(seed), 7)
    noisy = noise(key_list[0], (TOKENS, D), 1.0, 6.0, ((0, 16),))
    probes = draw_probes(jax.random.fold_in(key_list[6], 71), 0)
    w_qkv = noise(key_list[2], (D, 3 * D), D ** -0.5, 0.1875, ((1, 16),))
    w_out = noise(key_list[3], (D, D), D ** -0.5, 0.1875, ((0, 16),))
    w_mod = noise(key_list[4], (FREQ_DIM, 3 * D), FREQ_DIM ** -0.5, 0.375)
    timestep = jax.random.randint(key_list[5], (1,), 0, 1000).astype(jnp.int32)
    return dict(noisy=noisy, probes=probes, w_qkv=w_qkv, w_out=w_out, w_mod=w_mod, timestep=timestep)


def rounded(value):
    return lax.optimization_barrier(value.astype(jnp.bfloat16)).astype(jnp.float32)

def modulation(timestep, w_mod, feat_width):
    half_dim = w_mod.shape[0] // 2
    freq_index = jnp.arange(half_dim, dtype=jnp.float32)
    frequency = jnp.exp(-math.log(10000.0) * freq_index / half_dim)
    angles = timestep[0].astype(jnp.float32) * frequency
    embedding = jnp.concatenate([jnp.cos(angles), jnp.sin(angles)])
    modulated = jnp.dot(jax.nn.silu(embedding)[None, :], w_mod.astype(jnp.float32), precision=lax.Precision.HIGHEST)[0]
    return (modulated[:feat_width], modulated[feat_width:2 * feat_width], modulated[2 * feat_width:])

def normalize(noisy):
    values_f = noisy.astype(jnp.float32)
    centered = values_f - lax.optimization_barrier(jnp.mean(values_f, axis=-1, keepdims=True))
    deviation = jnp.sqrt(lax.optimization_barrier(jnp.mean(centered * centered, axis=-1, keepdims=True)) + 1e-06)
    return (centered / deviation, deviation)

def norm_tangent(field, normed, deviation):
    mean_part = lax.optimization_barrier(jnp.mean(field, axis=-1, keepdims=True))
    along = lax.optimization_barrier(jnp.mean(field * normed, axis=-1, keepdims=True))
    return (field - mean_part - normed * along) / deviation

def frame_probs(queries, key_rows):
    score_scale = HEAD_DIM ** (-0.5)
    scores = jnp.einsum('qhd,khd->hqk', queries, key_rows) * score_scale
    expon = jnp.exp(scores - lax.optimization_barrier(jnp.max(scores, axis=-1, keepdims=True)))
    return rounded(expon / lax.optimization_barrier(jnp.sum(expon, axis=-1, keepdims=True)))

def frame_tangent(primal_frame, tangent_frame):
    score_scale = HEAD_DIM ** (-0.5)
    queries = primal_frame[:, :, 0].astype(jnp.float32)
    key_rows = primal_frame[:, :, 1].astype(jnp.float32)
    values = primal_frame[:, :, 2].astype(jnp.float32)
    d_query = tangent_frame[:, :, 0].astype(jnp.float32)
    d_key = tangent_frame[:, :, 1].astype(jnp.float32)
    d_value = tangent_frame[:, :, 2].astype(jnp.float32)
    p_float = frame_probs(queries, key_rows)
    base_out = jnp.einsum('hqk,khd->qhd', p_float, values)
    d_scores = (jnp.einsum('qhd,khd->hqk', d_query, key_rows) + jnp.einsum('qhd,khd->hqk', queries, d_key)) * score_scale
    row_sum = lax.optimization_barrier(jnp.sum(p_float * d_scores, axis=-1))
    mixed_p = rounded(p_float * d_scores)
    out_tan = jnp.einsum('hqk,khd->qhd', mixed_p, values) + jnp.einsum('hqk,khd->qhd', p_float, d_value)
    out_tan = out_tan - jnp.transpose(row_sum)[:, :, None] * base_out
    return out_tan.astype(jnp.bfloat16)

def frame_adjoint(primal_frame, cot_frame):
    score_scale = HEAD_DIM ** (-0.5)
    queries = primal_frame[:, :, 0].astype(jnp.float32)
    key_rows = primal_frame[:, :, 1].astype(jnp.float32)
    values = primal_frame[:, :, 2].astype(jnp.float32)
    cot_f = cot_frame.astype(jnp.float32)
    p_float = frame_probs(queries, key_rows)
    d_value = jnp.einsum('hqk,qhd->khd', p_float, cot_f).astype(jnp.bfloat16)
    d_probs = jnp.einsum('qhd,khd->hqk', cot_f, values)
    row_dot = lax.optimization_barrier(jnp.sum(p_float * d_probs, axis=-1, keepdims=True))
    scaled_grad = rounded(p_float * (d_probs - row_dot) * score_scale)
    d_query = jnp.einsum('hqk,khd->qhd', scaled_grad, key_rows).astype(jnp.bfloat16)
    d_key = jnp.einsum('hqk,qhd->khd', scaled_grad, queries).astype(jnp.bfloat16)
    return jnp.stack([d_query, d_key, d_value], axis=2)

def reference(noisy, probes, w_qkv, w_out, w_mod, timestep):
    shift_mod, scale_mod, gate_mod = modulation(timestep, w_mod, D)
    normed, deviation = normalize(noisy)
    hidden = (normed * (1.0 + scale_mod) + shift_mod).astype(jnp.bfloat16)
    primal = jnp.dot(hidden.astype(jnp.float32), w_qkv.astype(jnp.float32), preferred_element_type=jnp.float32).astype(jnp.bfloat16)
    primal_five = primal.reshape(FRAMES, FRAME_TOK, HEADS, 3, HEAD_DIM)

    def one_probe(probe_b):
        vector = probe_b.astype(jnp.float32)
        d_hidden = (norm_tangent(vector, normed, deviation) * (1.0 + scale_mod)).astype(jnp.bfloat16)
        tangent = jnp.dot(d_hidden.astype(jnp.float32), w_qkv.astype(jnp.float32), preferred_element_type=jnp.float32).astype(jnp.bfloat16)
        tangent_five = tangent.reshape(FRAMES, FRAME_TOK, HEADS, 3, HEAD_DIM)
        d_attn = lax.map(lambda frame_pair: frame_tangent(frame_pair[0], frame_pair[1]), (primal_five, tangent_five))
        d_attn = d_attn.reshape(TOKENS, D)
        update = vector + gate_mod * jnp.dot(d_attn.astype(jnp.float32), w_out.astype(jnp.float32), preferred_element_type=jnp.float32)
        gated = (gate_mod * update).astype(jnp.bfloat16)
        cotangent = jnp.dot(gated.astype(jnp.float32), w_out.T.astype(jnp.float32), preferred_element_type=jnp.float32).astype(jnp.bfloat16)
        cot_four = cotangent.reshape(FRAMES, FRAME_TOK, HEADS, HEAD_DIM)
        grads = lax.map(lambda frame_pair: frame_adjoint(frame_pair[0], frame_pair[1]), (primal_five, cot_four))
        grads = grads.reshape(TOKENS, 3 * D)
        d_bar = jnp.dot(grads.astype(jnp.float32), w_qkv.T.astype(jnp.float32), preferred_element_type=jnp.float32)
        return update + norm_tangent((1.0 + scale_mod) * d_bar, normed, deviation)
    pulled = lax.map(one_probe, probes)
    flat_rows = pulled.reshape(PROBES, TOKENS * D)
    gram_total = jnp.dot(flat_rows.astype(jnp.float32), flat_rows.T.astype(jnp.float32), precision=lax.Precision.HIGHEST, preferred_element_type=jnp.float32) / (TOKENS * D)
    lower_tri = jnp.linalg.cholesky(gram_total)
    solved = lax.linalg.triangular_solve(lower_tri, flat_rows, left_side=True, lower=True)
    return (solved.reshape(PROBES, TOKENS, D), jnp.transpose(lower_tri))
```

```python
import functools
import math

import jax
import jax.numpy as jnp
from jax import lax
from jax.experimental import pallas as pl
from jax.experimental.pallas import tpu as pltpu
from jax.sharding import Mesh
from jax.sharding import PartitionSpec as P

HEAD_DIM = 72
LANES = 128
FRAMES = 2
SEQ = ("frame", "part")
PROBE = ("z", "core")
MIB = 1024 * 1024
STEP = 4
NT = (((1,), (1,)), ((), ()))
NN = (((1,), (0,)), ((), ()))
BF = jnp.bfloat16
F32 = jnp.float32


def mm(a, b, dims=NN):
    return lax.dot_general(a, b, dims, preferred_element_type=F32)


def exact(a, b, dims=NN):
    return lax.dot_general(
        a, b, dims, precision=lax.Precision.HIGHEST, preferred_element_type=F32
    )


def eye(n):
    row = lax.broadcasted_iota(jnp.int32, (n, n), 0)
    col = lax.broadcasted_iota(jnp.int32, (n, n), 1)
    return jnp.where(row == col, 1.0, 0.0)


def flip(a):
    return mm(eye(a.shape[1]).astype(BF), a, NT).astype(BF)


def modulation(timestep, w_mod, feat_width):
    half_dim = w_mod.shape[0] // 2
    freq_index = jnp.arange(half_dim, dtype=jnp.float32)
    frequency = jnp.exp(-math.log(10000.0) * freq_index / half_dim)
    angles = timestep[0].astype(jnp.float32) * frequency
    embedding = jnp.concatenate([jnp.cos(angles), jnp.sin(angles)])
    modulated = jnp.dot(
        jax.nn.silu(embedding)[None, :], w_mod.astype(jnp.float32), precision=lax.Precision.HIGHEST
    )
    return modulated.reshape(3, feat_width)


def normalize(values_f):
    centered = values_f - jnp.mean(values_f, axis=-1, keepdims=True)
    inverse = 1.0 / jnp.sqrt(jnp.mean(centered * centered, axis=-1, keepdims=True) + 1e-06)
    return centered * inverse, inverse


def norm_tangent(field, normed, inverse):
    mean_part = jnp.mean(field, axis=-1, keepdims=True)
    along = jnp.mean(field * normed, axis=-1, keepdims=True)
    return (field - mean_part - normed * along) * inverse


def fetch(pairs, sems):
    copies = [pltpu.make_async_copy(a, b, sems.at[i]) for i, (a, b) in enumerate(pairs)]
    for copy in copies:
        copy.start()
    return copies


def copies_kernel(noisy, probe, out, sems):
    count = out.shape[0]
    pairs = [(noisy, out.at[j, 0]) for j in range(count)]
    pairs += [(probe.at[0], out.at[j, 1]) for j in range(count)]
    for copy in fetch(pairs, sems):
        copy.wait()


def head_forward(hidden, d_hidden, weights, primal, probs):
    c = HEAD_DIM ** (-0.5)
    q, k, v = [mm(hidden, weights[i], NT).astype(BF) for i in range(3)]
    dq, dk, dv = [mm(d_hidden, weights[i], NT).astype(BF) for i in range(3)]
    scores = mm(q, k, NT) * c
    expon = jnp.exp(scores - jnp.max(scores, axis=-1, keepdims=True))
    p = (expon / jnp.sum(expon, axis=-1, keepdims=True)).astype(BF)
    d_scores = (mm(dq, k, NT) + mm(q, dk, NT)) * c
    mixed = p.astype(F32) * d_scores
    row_sum = jnp.sum(mixed, axis=-1, keepdims=True)
    out = mm(mixed.astype(BF), v) + mm(p, dv) - row_sum * mm(p, v)
    probs[...] = p
    for i, value in enumerate((q, k, v)):
        primal[i] = value
    return mm(out.astype(BF), weights[3])


def near_kernel(gath, weights, mods, hidden, d_hidden, term, primal, probs):
    blocks, _, rows, _ = gath.shape
    scale = 1.0 + mods[1:2, :]
    shift = mods[0:1, :]

    def block(i, carry):
        normed, inverse = normalize(gath[i, 0].astype(F32))
        at = pl.ds(pl.multiple_of(i * rows, rows), rows)
        hidden[at, :] = (normed * scale + shift).astype(BF)
        field = norm_tangent(gath[i, 1].astype(F32), normed, inverse)
        d_hidden[at, :] = (field * scale).astype(BF)
        return carry

    lax.fori_loop(0, blocks, block, 0, unroll=2)
    term[...] = head_forward(hidden[...], d_hidden[...], weights, primal, probs)


def far_kernel(hidden, d_hidden, weights, term, parts, primal, probs):
    total = term[...] + head_forward(hidden[...], d_hidden[...], weights, primal, probs)
    parts[...] = total.astype(BF).reshape(parts.shape)


def update_kernel(parts, probe, mods, gated, update):
    total = parts[0].astype(F32)
    for j in range(1, parts.shape[0]):
        total = total + parts[j].astype(F32)
    gate = mods[2:3, :]
    fresh = probe[0].astype(F32) + gate * total
    update[...] = fresh
    value = (gate * fresh).astype(BF)
    for j in range(gated.shape[0]):
        gated[j] = value


def adjoint_kernel(gated, near, near_primal, near_probs, far, far_primal, far_probs, parts):
    c = HEAD_DIM ** (-0.5)
    blocks, rows, width = gated.shape
    whole = gated[...].reshape(blocks * rows, width)
    total = None
    for weights, primal, probs in (
        (near, near_primal, near_probs),
        (far, far_primal, far_probs),
    ):
        co = mm(whole, weights[3], NT).astype(BF)
        q, k, v = primal[0], primal[1], primal[2]
        p = probs[...]
        p_float = p.astype(F32)
        d_probs = mm(co, v, NT)
        row_dot = jnp.sum(p_float * d_probs, axis=-1, keepdims=True)
        scaled = (p_float * (d_probs - row_dot) * c).astype(BF)
        grads = (mm(scaled, k), mm(flip(scaled), q), mm(flip(p), co))
        for i, grad in enumerate(grads):
            term = mm(grad.astype(BF), weights[i])
            total = term if total is None else total + term
    parts[...] = total.astype(BF).reshape(parts.shape)


def pulled_kernel(parts, update, noisy, mods, pulled):
    total = parts[0].astype(F32)
    for j in range(1, parts.shape[0]):
        total = total + parts[j].astype(F32)
    normed, inverse = normalize(noisy[...].astype(F32))
    value = update[...] + norm_tangent((1.0 + mods[1:2, :]) * total, normed, inverse)
    pulled[:, 0, :] = value


def gram_kernel(scale, by_probe, copies, flat):
    rows = by_probe[:, 0, :]
    flat[...] = rows
    gram = exact(rows, rows, NT) * scale
    n = gram.shape[0]
    width = LANES // n
    high = n // width
    packed = jnp.concatenate([gram[i * high : (i + 1) * high] for i in range(width)], axis=1)
    for j in range(copies.shape[0]):
        copies[j] = packed


def tree_sum(terms):
    while len(terms) > 1:
        terms = [terms[i] + terms[i + 1] for i in range(0, len(terms), 2)]
    return terms[0]


def total_kernel(arrived, copies):
    total = tree_sum([arrived[j] for j in range(arrived.shape[0])])
    for j in range(copies.shape[0]):
        copies[j] = total


def solve_kernel(arrived, flat, factor, solved):
    packed = tree_sum([arrived[j] for j in range(arrived.shape[0])])
    n = flat.shape[0]
    width = LANES // n
    a = jnp.concatenate([packed[:, i * n : (i + 1) * n] for i in range(width)], axis=0)
    both = jnp.concatenate([a, eye(n)], axis=1)
    row = lax.broadcasted_iota(jnp.int32, both.shape, 0)
    col = lax.broadcasted_iota(jnp.int32, both.shape, 1)
    wide = (1, both.shape[1])
    for j in range(0, n, STEP):
        span = range(STEP)
        tops = [both[j + i : j + i + 1, :] for i in span]
        sides = [jnp.broadcast_to(both[:, j + i : j + i + 1], both.shape) for i in span]
        corner = [
            [jnp.broadcast_to(tops[i][:, j + k : j + k + 1], wide) for k in span] for i in span
        ]
        change = jnp.zeros_like(both)
        for i in span:
            inverse = 1.0 / corner[i][i]
            for k in range(i + 1, STEP):
                ratio = corner[i][k] * inverse
                tops[k] = tops[k] - ratio * tops[i]
                sides[k] = sides[k] - ratio * sides[i]
                for m in range(k, STEP):
                    corner[k][m] = corner[k][m] - ratio * corner[i][m]
            change = change + sides[i] * (tops[i] * inverse)
        below = both - jnp.where(row >= j + STEP, change, 0.0)
        for i in span:
            below = jnp.where(row == j + i, tops[i], below)
        both = below
    pivots = jnp.sum(jnp.where(row == col, both, 0.0), axis=1, keepdims=True)
    both = both / jnp.sqrt(pivots)
    factor[...] = jnp.where(col >= row, both, 0.0)[:, :n]
    rows = exact(both[:, n:], flat[...])
    half = solved.shape[2]
    for i in range(2):
        solved[:, i, :] = rows[:, i * half : (i + 1) * half].astype(BF)


def basis_kernel(halves, basis):
    half = halves.shape[2]
    for i in range(2):
        basis[0, :, i * half : (i + 1) * half] = halves[:, i, :].astype(F32)


HBM = pl.BlockSpec(memory_space=pl.ANY)
LOCAL = pl.BlockSpec(memory_space=pltpu.VMEM)


def call(
    kernel, out_shape, *args, where=None, out_specs=None, scratch=(), flops=0, moved=0, limit=8
):
    return pl.pallas_call(
        kernel,
        out_shape=out_shape,
        in_specs=where or [LOCAL] * len(args),
        out_specs=out_specs or jax.tree.map(lambda _: LOCAL, out_shape),
        scratch_shapes=list(scratch),
        compiler_params=pltpu.CompilerParams(vmem_limit_bytes=limit * MIB),
        cost_estimate=pl.CostEstimate(flops=flops, bytes_accessed=moved, transcendentals=0),
    )(*args)


def exchange(blocks, axis):
    return lax.all_to_all(blocks, axis, split_axis=0, concat_axis=0, tiled=True)


def shards(noisy, probes, w_qkv, w_out, w_mod, timestep):
    rows, width = noisy.shape
    parts, frames, cores, chips = [lax.axis_size(n) for n in ("part", "frame", "core", "z")]
    seq_count = parts * frames
    probe_count = cores * chips
    frame_rows = parts * rows

    outgoing = call(
        copies_kernel,
        jax.ShapeDtypeStruct((parts, 2, rows, width), BF),
        noisy,
        probes,
        out_specs=HBM,
        scratch=(pltpu.SemaphoreType.DMA((2 * parts,)),),
        moved=2 * 10**6,
        limit=60,
    )
    gath = exchange(outgoing, "part")
    near = jnp.concatenate([w_qkv.T, w_out], axis=0).reshape(4, HEAD_DIM, width)
    half = seq_count - seq_count // 4
    far = lax.ppermute(near, SEQ, [(i, i ^ half) for i in range(seq_count)])
    mods = modulation(timestep, w_mod, width)

    part_sums = jax.ShapeDtypeStruct((parts, rows, width), BF)
    tokens = jax.ShapeDtypeStruct((frame_rows, width), BF)
    kept = (
        jax.ShapeDtypeStruct((3, frame_rows, HEAD_DIM), BF),
        jax.ShapeDtypeStruct((frame_rows, frame_rows), BF),
    )
    hidden, d_hidden, term, near_primal, near_probs = call(
        near_kernel,
        (tokens, tokens, jax.ShapeDtypeStruct((frame_rows, width), F32)) + kept,
        gath,
        near,
        mods,
        flops=10**9,
        moved=6 * 10**6,
        limit=24,
    )
    sums, far_primal, far_probs = call(
        far_kernel,
        (part_sums,) + kept,
        hidden,
        d_hidden,
        far,
        term,
        flops=10**9,
        moved=4 * 10**6,
        limit=24,
    )
    sums = exchange(sums, "part")
    gated, update = call(
        update_kernel,
        (part_sums, jax.ShapeDtypeStruct((rows, width), F32)),
        sums,
        probes,
        mods,
        moved=10**6,
    )
    gated = exchange(gated, "part")
    sums = call(
        adjoint_kernel,
        part_sums,
        gated,
        near,
        near_primal,
        near_probs,
        far,
        far_primal,
        far_probs,
        flops=2 * 10**9,
        moved=5 * 10**6,
        limit=24,
    )
    sums = exchange(sums, "part")
    by_row = jax.ShapeDtypeStruct((rows, 1, width), F32)
    pulled = call(pulled_kernel, by_row, sums, update, noisy, mods, moved=10**6)
    sub_count = rows // probe_count
    by_probe = exchange(pulled, PROBE).reshape(probe_count, 1, sub_count * width)
    high = probe_count * probe_count // LANES

    def blocks_of(count):
        return jax.ShapeDtypeStruct((count, high, LANES), F32)

    grams, flat = call(
        functools.partial(gram_kernel, 1.0 / float(seq_count * rows * width)),
        (blocks_of(cores * seq_count), jax.ShapeDtypeStruct((probe_count, sub_count * width), F32)),
        by_probe,
        moved=10**5,
    )
    grams = exchange(grams, ("core",) + SEQ)
    grams = call(total_kernel, blocks_of(chips), grams, moved=10**5)
    factor, solved = call(
        solve_kernel,
        (
            jax.ShapeDtypeStruct((probe_count, probe_count), F32),
            jax.ShapeDtypeStruct((rows, 2, width // 2), BF),
        ),
        exchange(grams, "z"),
        flat,
        moved=3 * 10**5,
    )
    halves = exchange(solved, PROBE)
    basis = call(
        basis_kernel, jax.ShapeDtypeStruct((1, rows, width), F32), halves, moved=3 * 10**5
    )
    return basis, factor


def solution(mesh):
    split = Mesh(
        mesh.devices.reshape(
            mesh.shape["probe"] // 2, 2, FRAMES, mesh.shape["seq"] // FRAMES
        ),
        PROBE + SEQ,
    )
    placed = (P(SEQ, None), P(PROBE, SEQ, None), P(None, SEQ), P(SEQ, None), P(), P())
    return jax.shard_map(
        shards,
        mesh=split,
        in_specs=placed,
        out_specs=(P(PROBE, SEQ, None), P()),
        check_vma=False,
    )
```

```python
import functools
import math

import jax
import jax.numpy as jnp
from jax import lax
from jax.experimental import pallas as pl
from jax.experimental.pallas import tpu as pltpu
from jax.sharding import Mesh
from jax.sharding import PartitionSpec as P

HEAD_DIM = 72
LANES = 128
FRAMES = 2
SEQ = ("frame", "part")
PROBE = ("z", "core")
MIB = 1024 * 1024
STEP = 4
NT = (((1,), (1,)), ((), ()))
NN = (((1,), (0,)), ((), ()))
BF = jnp.bfloat16
F32 = jnp.float32


def mm(a, b, dims=NN):
    return lax.dot_general(a, b, dims, preferred_element_type=F32)


def exact(a, b, dims=NN):
    return lax.dot_general(
        a, b, dims, precision=lax.Precision.HIGHEST, preferred_element_type=F32
    )


def eye(n):
    row = lax.broadcasted_iota(jnp.int32, (n, n), 0)
    col = lax.broadcasted_iota(jnp.int32, (n, n), 1)
    return jnp.where(row == col, 1.0, 0.0)


def flip(a):
    return mm(eye(a.shape[1]).astype(BF), a, NT).astype(BF)


def modulation(timestep, w_mod, feat_width):
    half_dim = w_mod.shape[0] // 2
    freq_index = jnp.arange(half_dim, dtype=jnp.float32)
    frequency = jnp.exp(-math.log(10000.0) * freq_index / half_dim)
    angles = timestep[0].astype(jnp.float32) * frequency
    embedding = jnp.concatenate([jnp.cos(angles), jnp.sin(angles)])
    modulated = jnp.dot(
        jax.nn.silu(embedding)[None, :], w_mod.astype(jnp.float32), precision=lax.Precision.HIGHEST
    )
    return modulated.reshape(3, feat_width)


def normalize(values_f):
    centered = values_f - jnp.mean(values_f, axis=-1, keepdims=True)
    inverse = 1.0 / jnp.sqrt(jnp.mean(centered * centered, axis=-1, keepdims=True) + 1e-06)
    return centered * inverse, inverse


def norm_tangent(field, normed, inverse):
    mean_part = jnp.mean(field, axis=-1, keepdims=True)
    along = jnp.mean(field * normed, axis=-1, keepdims=True)
    return (field - mean_part - normed * along) * inverse


def fetch(pairs, sems):
    copies = [pltpu.make_async_copy(a, b, sems.at[i]) for i, (a, b) in enumerate(pairs)]
    for copy in copies:
        copy.start()
    return copies


def copies_kernel(noisy, probe, out, sems):
    count = out.shape[0]
    pairs = [(noisy, out.at[j, 0]) for j in range(count)]
    pairs += [(probe.at[0], out.at[j, 1]) for j in range(count)]
    for copy in fetch(pairs, sems):
        copy.wait()


def thirds(value):
    return [value[:, i * HEAD_DIM : (i + 1) * HEAD_DIM].astype(BF) for i in range(3)]


def project_in(weights):
    return weights[pl.ds(0, 3 * HEAD_DIM), :]


def head_forward(tokens, flat_weights, weights, primal, probs):
    c = HEAD_DIM ** (-0.5)
    count = tokens.shape[0] // 2
    projected = mm(tokens[...], project_in(flat_weights), NT)
    q, k, v = thirds(projected[:count])
    dq, dk, dv = thirds(projected[count:])
    scores = mm(q, k, NT) * c
    expon = jnp.exp(scores - jnp.max(scores, axis=-1, keepdims=True))
    p = (expon / jnp.sum(expon, axis=-1, keepdims=True)).astype(BF)
    d_scores = (mm(dq, k, NT) + mm(q, dk, NT)) * c
    mixed = p.astype(F32) * d_scores
    row_sum = jnp.sum(mixed, axis=-1, keepdims=True)
    out = mm(mixed.astype(BF), v) + mm(p, dv) - row_sum * mm(p, v)
    probs[...] = p
    for i, value in enumerate((q, k, v)):
        primal[i] = value
    return mm(out.astype(BF), weights[3])


def near_kernel(gath, flat_weights, weights, mods, tokens, term, primal, probs):
    blocks, _, rows, _ = gath.shape
    scale = 1.0 + mods[1:2, :]
    shift = mods[0:1, :]
    for i in range(blocks):
        normed, inverse = normalize(gath[i, 0].astype(F32))
        tokens[pl.ds(i * rows, rows), :] = (normed * scale + shift).astype(BF)
        field = norm_tangent(gath[i, 1].astype(F32), normed, inverse)
        tokens[pl.ds((blocks + i) * rows, rows), :] = (field * scale).astype(BF)
    term[...] = head_forward(tokens, flat_weights, weights, primal, probs)


def far_kernel(tokens, flat_weights, weights, term, parts, primal, probs):
    total = term[...] + head_forward(tokens, flat_weights, weights, primal, probs)
    parts[...] = total.astype(BF).reshape(parts.shape)


def update_kernel(parts, probe, mods, gated, update):
    total = parts[0].astype(F32)
    for j in range(1, parts.shape[0]):
        total = total + parts[j].astype(F32)
    gate = mods[2:3, :]
    fresh = probe[0].astype(F32) + gate * total
    update[...] = fresh
    value = (gate * fresh).astype(BF)
    for j in range(gated.shape[0]):
        gated[j] = value


def adjoint_kernel(
    gated, near_flat, near, near_primal, near_probs, far_flat, far, far_primal, far_probs, parts
):
    c = HEAD_DIM ** (-0.5)
    blocks, rows, width = gated.shape
    whole = gated[...].reshape(blocks * rows, width)
    total = None
    for flat_weights, weights, primal, probs in (
        (near_flat, near, near_primal, near_probs),
        (far_flat, far, far_primal, far_probs),
    ):
        co = mm(whole, weights[3], NT).astype(BF)
        q, k, v = primal[0], primal[1], primal[2]
        p = probs[...]
        p_float = p.astype(F32)
        d_probs = mm(co, v, NT)
        row_dot = jnp.sum(p_float * d_probs, axis=-1, keepdims=True)
        scaled = (p_float * (d_probs - row_dot) * c).astype(BF)
        grads = (mm(scaled, k), mm(flip(scaled), q), mm(flip(p), co))
        grads = jnp.concatenate(grads, axis=1).astype(BF)
        term = mm(grads, project_in(flat_weights))
        total = term if total is None else total + term
    parts[...] = total.astype(BF).reshape(parts.shape)


def pulled_kernel(parts, update, noisy, mods, pulled, lost):
    total = parts[0].astype(F32)
    for j in range(1, parts.shape[0]):
        total = total + parts[j].astype(F32)
    normed, inverse = normalize(noisy[...].astype(F32))
    value = update[...] + norm_tangent((1.0 + mods[1:2, :]) * total, normed, inverse)
    rounded = value.astype(BF)
    lost[...] = value - rounded.astype(F32)
    pairs, each, _ = pulled.shape
    for i in range(pairs):
        pulled[i] = value[i * each : (i + 1) * each].astype(BF)


def gram_kernel(scale, core, mine, other, copies, rows):
    first = core[0] == 0
    for i in range(mine.shape[0]):
        rows[2 * i] = jnp.where(first, mine[i], other[i])
        rows[2 * i + 1] = jnp.where(first, other[i], mine[i])
    each = [rows[:, t, :] for t in range(rows.shape[1])]
    gram = sum(mm(row, row, NT) for row in each) * scale
    n = gram.shape[0]
    width = LANES // n
    high = n // width
    packed = jnp.concatenate([gram[i * high : (i + 1) * high] for i in range(width)], axis=1)
    for j in range(copies.shape[0]):
        copies[j] = packed


def tree_sum(terms):
    while len(terms) > 1:
        terms = [terms[i] + terms[i + 1] for i in range(0, len(terms), 2)]
    return terms[0]


def total_kernel(arrived, copies):
    total = tree_sum([arrived[j] for j in range(arrived.shape[0])])
    for j in range(copies.shape[0]):
        copies[j] = total


def picked(n, core):
    row = lax.broadcasted_iota(jnp.int32, (n // 2, n), 0)
    col = lax.broadcasted_iota(jnp.int32, (n // 2, n), 1)
    return jnp.where(col == 2 * row + core, 1.0, 0.0)


def solve_kernel(place, arrived, rows, lost, factor, solved, rest):
    packed = tree_sum([arrived[j] for j in range(arrived.shape[0])])
    n = factor.shape[0]
    width = LANES // n
    a = jnp.concatenate([packed[:, i * n : (i + 1) * n] for i in range(width)], axis=0)
    both = jnp.concatenate([a, eye(n)], axis=1)
    row = lax.broadcasted_iota(jnp.int32, both.shape, 0)
    col = lax.broadcasted_iota(jnp.int32, both.shape, 1)
    wide = (1, both.shape[1])
    for j in range(0, n, STEP):
        span = range(STEP)
        tops = [both[j + i : j + i + 1, :] for i in span]
        sides = [jnp.broadcast_to(both[:, j + i : j + i + 1], both.shape) for i in span]
        corner = [
            [jnp.broadcast_to(tops[i][:, j + k : j + k + 1], wide) for k in span] for i in span
        ]
        change = jnp.zeros_like(both)
        for i in span:
            inverse = 1.0 / corner[i][i]
            for k in range(i + 1, STEP):
                ratio = corner[i][k] * inverse
                tops[k] = tops[k] - ratio * tops[i]
                sides[k] = sides[k] - ratio * sides[i]
                for m in range(k, STEP):
                    corner[k][m] = corner[k][m] - ratio * corner[i][m]
            change = change + sides[i] * (tops[i] * inverse)
        below = both - jnp.where(row >= j + STEP, change, 0.0)
        for i in span:
            below = jnp.where(row == j + i, tops[i], below)
        both = below
    pivots = jnp.sum(jnp.where(row == col, both, 0.0), axis=1, keepdims=True)
    both = both / jnp.sqrt(pivots)
    factor[...] = jnp.where(col >= row, both, 0.0)[:, :n]
    own = place[0] * 2 + place[1]
    square = jnp.where((row == own) & (col == own), both, 0.0)
    pivot = jnp.sum(jnp.sum(square, axis=0, keepdims=True), axis=1, keepdims=True)
    rest[...] = lost[...] * (1.0 / pivot)
    inverse = exact(picked(n, place[1]), both[:, n:])
    for t in range(rows.shape[1]):
        solved[:, t, :] = exact(inverse, rows[:, t, :].astype(F32)).astype(BF)


def basis_kernel(pairs, rest, basis):
    count, each, _ = pairs.shape
    for i in range(count):
        at = slice(i * each, (i + 1) * each)
        basis[0, at, :] = pairs[i].astype(F32) + rest[at, :]


HBM = pl.BlockSpec(memory_space=pl.ANY)
LOCAL = pl.BlockSpec(memory_space=pltpu.VMEM)
SCALAR = pl.BlockSpec(memory_space=pltpu.SMEM)


def call(
    kernel, out_shape, *args, where=None, out_specs=None, scratch=(), flops=0, moved=0, limit=8
):
    return pl.pallas_call(
        kernel,
        out_shape=out_shape,
        in_specs=where or [LOCAL] * len(args),
        out_specs=out_specs or jax.tree.map(lambda _: LOCAL, out_shape),
        scratch_shapes=list(scratch),
        compiler_params=pltpu.CompilerParams(vmem_limit_bytes=limit * MIB),
        cost_estimate=pl.CostEstimate(flops=flops, bytes_accessed=moved, transcendentals=0),
    )(*args)


def exchange(blocks, axis):
    return lax.all_to_all(blocks, axis, split_axis=0, concat_axis=0, tiled=True)


def shards(noisy, probes, w_qkv, w_out, w_mod, timestep):
    rows, width = noisy.shape
    parts, frames, cores, chips = [lax.axis_size(n) for n in ("part", "frame", "core", "z")]
    seq_count = parts * frames
    probe_count = cores * chips
    frame_rows = parts * rows

    outgoing = call(
        copies_kernel,
        jax.ShapeDtypeStruct((parts, 2, rows, width), BF),
        noisy,
        probes,
        out_specs=HBM,
        scratch=(pltpu.SemaphoreType.DMA((2 * parts,)),),
        moved=2 * 10**6,
        limit=60,
    )
    gath = exchange(outgoing, "part")
    near = jnp.concatenate([w_qkv.T, w_out], axis=0).reshape(4, HEAD_DIM, width)
    half = seq_count - seq_count // 4
    far = lax.ppermute(near, SEQ, [(i, i ^ half) for i in range(seq_count)])
    near_flat, far_flat = [w.reshape(4 * HEAD_DIM, width) for w in (near, far)]
    mods = modulation(timestep, w_mod, width)

    part_sums = jax.ShapeDtypeStruct((parts, rows, width), BF)
    kept = (
        jax.ShapeDtypeStruct((3, frame_rows, HEAD_DIM), BF),
        jax.ShapeDtypeStruct((frame_rows, frame_rows), BF),
    )
    tokens, term, near_primal, near_probs = call(
        near_kernel,
        (
            jax.ShapeDtypeStruct((2 * frame_rows, width), BF),
            jax.ShapeDtypeStruct((frame_rows, width), F32),
        )
        + kept,
        gath,
        near_flat,
        near,
        mods,
        flops=10**9,
        moved=6 * 10**6,
        limit=24,
    )
    sums, far_primal, far_probs = call(
        far_kernel,
        (part_sums,) + kept,
        tokens,
        far_flat,
        far,
        term,
        flops=10**9,
        moved=4 * 10**6,
        limit=24,
    )
    sums = exchange(sums, "part")
    gated, update = call(
        update_kernel,
        (part_sums, jax.ShapeDtypeStruct((rows, width), F32)),
        sums,
        probes,
        mods,
        moved=10**6,
    )
    gated = exchange(gated, "part")
    sums = call(
        adjoint_kernel,
        part_sums,
        gated,
        near_flat,
        near,
        near_primal,
        near_probs,
        far_flat,
        far,
        far_primal,
        far_probs,
        flops=2 * 10**9,
        moved=5 * 10**6,
        limit=24,
    )
    sums = exchange(sums, "part")
    pairs = jax.ShapeDtypeStruct((chips, rows // chips, width), BF)
    own_rows = jax.ShapeDtypeStruct((rows, width), F32)
    pulled, lost = call(
        pulled_kernel, (pairs, own_rows), sums, update, noisy, mods, moved=10**6
    )
    place = jnp.stack([lax.axis_index("z"), lax.axis_index("core")]).astype(jnp.int32)
    mine = exchange(pulled, "z")
    other = lax.ppermute(mine, "core", [(i, i ^ 1) for i in range(cores)])
    high = probe_count * probe_count // LANES

    def blocks_of(count):
        return jax.ShapeDtypeStruct((count, high, LANES), F32)

    grams, every = call(
        functools.partial(gram_kernel, 1.0 / float(seq_count * rows * width)),
        (
            blocks_of(seq_count),
            jax.ShapeDtypeStruct((probe_count, rows // chips, width), BF),
        ),
        place[1:],
        mine,
        other,
        where=[SCALAR, LOCAL, LOCAL],
        moved=10**5,
    )
    grams = exchange(grams, SEQ)
    grams = call(total_kernel, blocks_of(chips), grams, moved=10**5)
    factor, solved, rest = call(
        solve_kernel,
        (jax.ShapeDtypeStruct((probe_count, probe_count), F32), pairs, own_rows),
        place,
        exchange(grams, "z"),
        every,
        lost,
        where=[SCALAR] + [LOCAL] * 3,
        moved=3 * 10**5,
    )
    basis = call(
        basis_kernel,
        jax.ShapeDtypeStruct((1, rows, width), F32),
        exchange(solved, "z"),
        rest,
        moved=3 * 10**5,
    )
    return basis, factor


def solution(mesh):
    split = Mesh(
        mesh.devices.reshape(
            mesh.shape["probe"] // 2, 2, FRAMES, mesh.shape["seq"] // FRAMES
        ),
        PROBE + SEQ,
    )
    placed = (P(SEQ, None), P(PROBE, SEQ, None), P(None, SEQ), P(SEQ, None), P(), P())
    return jax.shard_map(
        shards,
        mesh=split,
        in_specs=placed,
        out_specs=(P(PROBE, SEQ, None), P()),
        check_vma=False,
    )
```

```python
import functools
import math

import jax
import jax.numpy as jnp
from jax import lax
from jax.experimental import pallas as pl
from jax.experimental.pallas import tpu as pltpu
from jax.sharding import Mesh
from jax.sharding import PartitionSpec as P

HEAD_DIM = 72
LANES = 128
FRAMES = 2
SEQ = ("frame", "part")
PROBE = ("z", "core")
MIB = 1024 * 1024
STEP = 4
NT = (((1,), (1,)), ((), ()))
NN = (((1,), (0,)), ((), ()))
BF = jnp.bfloat16
F32 = jnp.float32


def mm(a, b, dims=NN):
    return lax.dot_general(a, b, dims, preferred_element_type=F32)


def exact(a, b, dims=NN):
    return lax.dot_general(
        a, b, dims, precision=lax.Precision.HIGHEST, preferred_element_type=F32
    )


def eye(n):
    row = lax.broadcasted_iota(jnp.int32, (n, n), 0)
    col = lax.broadcasted_iota(jnp.int32, (n, n), 1)
    return jnp.where(row == col, 1.0, 0.0)


def flip(a):
    return mm(eye(a.shape[1]).astype(BF), a, NT).astype(BF)


def modulation(timestep, w_mod, feat_width):
    half_dim = w_mod.shape[0] // 2
    freq_index = jnp.arange(half_dim, dtype=jnp.float32)
    frequency = jnp.exp(-math.log(10000.0) * freq_index / half_dim)
    angles = timestep[0].astype(jnp.float32) * frequency
    embedding = jnp.concatenate([jnp.cos(angles), jnp.sin(angles)])
    modulated = jnp.dot(
        jax.nn.silu(embedding)[None, :], w_mod.astype(jnp.float32), precision=lax.Precision.HIGHEST
    )
    return modulated.reshape(3, feat_width)


def normalize(values_f):
    centered = values_f - jnp.mean(values_f, axis=-1, keepdims=True)
    inverse = 1.0 / jnp.sqrt(jnp.mean(centered * centered, axis=-1, keepdims=True) + 1e-06)
    return centered * inverse, inverse


def norm_tangent(field, normed, inverse):
    mean_part = jnp.mean(field, axis=-1, keepdims=True)
    along = jnp.mean(field * normed, axis=-1, keepdims=True)
    return (field - mean_part - normed * along) * inverse


def fetch(pairs, sems):
    copies = [pltpu.make_async_copy(a, b, sems.at[i]) for i, (a, b) in enumerate(pairs)]
    for copy in copies:
        copy.start()
    return copies


def copies_kernel(noisy, probe, out, staged, sems):
    count = out.shape[0]
    for copy in fetch([(noisy, staged.at[0]), (probe.at[0], staged.at[1])], sems):
        copy.wait()
    for copy in fetch([(staged, out.at[j]) for j in range(count)], sems.at[pl.ds(2, count)]):
        copy.wait()


def thirds(value):
    return [value[:, i * HEAD_DIM : (i + 1) * HEAD_DIM].astype(BF) for i in range(3)]


def project_in(weights):
    return weights[pl.ds(0, 3 * HEAD_DIM), :]


def head_forward(tokens, flat_weights, weights, primal, probs):
    c = HEAD_DIM ** (-0.5)
    count = tokens.shape[0] // 2
    projected = mm(tokens[...], project_in(flat_weights), NT)
    q, k, v = thirds(projected[:count])
    dq, dk, dv = thirds(projected[count:])
    scores = mm(q, k, NT) * c
    expon = jnp.exp(scores - jnp.max(scores, axis=-1, keepdims=True))
    p = (expon * (1.0 / jnp.sum(expon, axis=-1, keepdims=True))).astype(BF)
    d_scores = (mm(dq, k, NT) + mm(q, dk, NT)) * c
    mixed = p.astype(F32) * d_scores
    row_sum = jnp.sum(mixed, axis=-1, keepdims=True)
    out = mm(mixed.astype(BF), v) + mm(p, dv) - row_sum * mm(p, v)
    probs[...] = p
    for i, value in enumerate((q, k, v)):
        primal[i] = value
    return mm(out.astype(BF), weights[3])


def near_kernel(gath, flat_weights, weights, mods, tokens, term, primal, probs):
    blocks, _, rows, _ = gath.shape
    scale = 1.0 + mods[1:2, :]
    shift = mods[0:1, :]
    for i in range(blocks):
        normed, inverse = normalize(gath[i, 0].astype(F32))
        tokens[pl.ds(i * rows, rows), :] = (normed * scale + shift).astype(BF)
        field = norm_tangent(gath[i, 1].astype(F32), normed, inverse)
        tokens[pl.ds((blocks + i) * rows, rows), :] = (field * scale).astype(BF)
    term[...] = head_forward(tokens, flat_weights, weights, primal, probs)


def far_kernel(tokens, flat_weights, weights, term, parts, primal, probs):
    total = term[...] + head_forward(tokens, flat_weights, weights, primal, probs)
    parts[...] = total.astype(BF).reshape(parts.shape)


def update_kernel(parts, probe, mods, gated, update):
    total = parts[0].astype(F32)
    for j in range(1, parts.shape[0]):
        total = total + parts[j].astype(F32)
    gate = mods[2:3, :]
    fresh = probe[0].astype(F32) + gate * total
    update[...] = fresh
    value = (gate * fresh).astype(BF)
    for j in range(gated.shape[0]):
        gated[j] = value


def adjoint_kernel(
    gated, near_flat, near, near_primal, near_probs, far_flat, far, far_primal, far_probs, parts
):
    c = HEAD_DIM ** (-0.5)
    blocks, rows, width = gated.shape
    whole = gated[...].reshape(blocks * rows, width)
    total = None
    for flat_weights, weights, primal, probs in (
        (near_flat, near, near_primal, near_probs),
        (far_flat, far, far_primal, far_probs),
    ):
        co = mm(whole, weights[3], NT).astype(BF)
        q, k, v = primal[0], primal[1], primal[2]
        p = probs[...]
        p_float = p.astype(F32)
        d_probs = mm(co, v, NT)
        row_dot = jnp.sum(p_float * d_probs, axis=-1, keepdims=True)
        scaled = (p_float * (d_probs - row_dot) * c).astype(BF)
        grads = (mm(scaled, k), mm(flip(scaled), q), mm(flip(p), co))
        grads = jnp.concatenate(grads, axis=1).astype(BF)
        term = mm(grads, project_in(flat_weights))
        total = term if total is None else total + term
    parts[...] = total.astype(BF).reshape(parts.shape)


def pulled_kernel(parts, update, noisy, mods, pulled, lost):
    total = parts[0].astype(F32)
    for j in range(1, parts.shape[0]):
        total = total + parts[j].astype(F32)
    normed, inverse = normalize(noisy[...].astype(F32))
    value = update[...] + norm_tangent((1.0 + mods[1:2, :]) * total, normed, inverse)
    rounded = value.astype(BF)
    lost[...] = value - rounded.astype(F32)
    pairs, each, _ = pulled.shape
    for i in range(pairs):
        pulled[i] = value[i * each : (i + 1) * each].astype(BF)


def gram_kernel(scale, mine, other, copies, rows):
    first = lax.axis_index("core") == 0
    for i in range(mine.shape[0]):
        rows[2 * i] = jnp.where(first, mine[i], other[i])
        rows[2 * i + 1] = jnp.where(first, other[i], mine[i])
    each = [rows[:, t, :] for t in range(rows.shape[1])]
    gram = sum(mm(row, row, NT) for row in each) * scale
    n = gram.shape[0]
    width = LANES // n
    high = n // width
    packed = jnp.concatenate([gram[i * high : (i + 1) * high] for i in range(width)], axis=1)
    for j in range(copies.shape[0]):
        copies[j] = packed


def tree_sum(terms):
    while len(terms) > 1:
        terms = [terms[i] + terms[i + 1] for i in range(0, len(terms), 2)]
    return terms[0]


def total_kernel(arrived, copies):
    total = tree_sum([arrived[j] for j in range(arrived.shape[0])])
    for j in range(copies.shape[0]):
        copies[j] = total


def picked(n, core):
    row = lax.broadcasted_iota(jnp.int32, (n // 2, n), 0)
    col = lax.broadcasted_iota(jnp.int32, (n // 2, n), 1)
    return jnp.where(col == 2 * row + core, 1.0, 0.0)


def solve_kernel(arrived, rows, lost, factor, solved, rest):
    packed = tree_sum([arrived[j] for j in range(arrived.shape[0])])
    n = factor.shape[0]
    width = LANES // n
    a = jnp.concatenate([packed[:, i * n : (i + 1) * n] for i in range(width)], axis=0)
    both = jnp.concatenate([a, eye(n)], axis=1)
    row = lax.broadcasted_iota(jnp.int32, both.shape, 0)
    col = lax.broadcasted_iota(jnp.int32, both.shape, 1)
    wide = (1, both.shape[1])
    for j in range(0, n, STEP):
        span = range(STEP)
        tops = [both[j + i : j + i + 1, :] for i in span]
        sides = [jnp.broadcast_to(both[:, j + i : j + i + 1], both.shape) for i in span]
        corner = [
            [jnp.broadcast_to(tops[i][:, j + k : j + k + 1], wide) for k in span] for i in span
        ]
        change = jnp.zeros_like(both)
        for i in span:
            inverse = 1.0 / corner[i][i]
            for k in range(i + 1, STEP):
                ratio = corner[i][k] * inverse
                tops[k] = tops[k] - ratio * tops[i]
                sides[k] = sides[k] - ratio * sides[i]
                for m in range(k, STEP):
                    corner[k][m] = corner[k][m] - ratio * corner[i][m]
            change = change + sides[i] * (tops[i] * inverse)
        below = both - jnp.where(row >= j + STEP, change, 0.0)
        for i in span:
            below = jnp.where(row == j + i, tops[i], below)
        both = below
    pivots = jnp.sum(jnp.where(row == col, both, 0.0), axis=1, keepdims=True)
    both = both / jnp.sqrt(pivots)
    factor[...] = jnp.where(col >= row, both, 0.0)[:, :n]
    core = lax.axis_index("core")
    own = lax.axis_index("z") * 2 + core
    square = jnp.where((row == own) & (col == own), both, 0.0)
    pivot = jnp.sum(jnp.sum(square, axis=0, keepdims=True), axis=1, keepdims=True)
    rest[...] = lost[...] * (1.0 / pivot)
    remains = both[:, n:]
    choice = picked(n, core).astype(BF)
    pieces = []
    for _ in range(3):
        piece = remains.astype(BF)
        pieces.append(mm(choice, piece))
        remains = remains - piece.astype(F32)
    pieces = jnp.concatenate(pieces, axis=0).astype(BF)
    for t in range(rows.shape[1]):
        product = mm(pieces, rows[:, t, :])
        high, middle, low = [product[i * n // 2 : (i + 1) * n // 2] for i in range(3)]
        solved[:, t, :] = (high + (middle + low)).astype(BF)


def basis_kernel(pairs, rest, basis):
    count, each, _ = pairs.shape
    for i in range(count):
        at = slice(i * each, (i + 1) * each)
        basis[0, at, :] = pairs[i].astype(F32) + rest[at, :]


HBM = pl.BlockSpec(memory_space=pl.ANY)
LOCAL = pl.BlockSpec(memory_space=pltpu.VMEM)


def call(
    kernel, out_shape, *args, where=None, out_specs=None, scratch=(), flops=0, moved=0, limit=8
):
    return pl.pallas_call(
        kernel,
        out_shape=out_shape,
        in_specs=where or [LOCAL] * len(args),
        out_specs=out_specs or jax.tree.map(lambda _: LOCAL, out_shape),
        scratch_shapes=list(scratch),
        compiler_params=pltpu.CompilerParams(vmem_limit_bytes=limit * MIB),
        cost_estimate=pl.CostEstimate(flops=flops, bytes_accessed=moved, transcendentals=0),
    )(*args)


def exchange(blocks, axis):
    return lax.all_to_all(blocks, axis, split_axis=0, concat_axis=0, tiled=True)


def shards(noisy, probes, w_qkv, w_out, w_mod, timestep):
    rows, width = noisy.shape
    parts, frames, cores, chips = [lax.axis_size(n) for n in ("part", "frame", "core", "z")]
    seq_count = parts * frames
    probe_count = cores * chips
    frame_rows = parts * rows

    outgoing = call(
        copies_kernel,
        jax.ShapeDtypeStruct((parts, 2, rows, width), BF),
        noisy,
        probes,
        where=[HBM, HBM],
        out_specs=HBM,
        scratch=(
            pltpu.VMEM((2, rows, width), BF),
            pltpu.SemaphoreType.DMA((2 + parts,)),
        ),
        moved=2 * 10**6,
        limit=60,
    )
    gath = exchange(outgoing, "part")
    near = jnp.concatenate([w_qkv.T, w_out], axis=0).reshape(4, HEAD_DIM, width)
    half = seq_count - seq_count // 4
    far = lax.ppermute(near, SEQ, [(i, i ^ half) for i in range(seq_count)])
    near_flat, far_flat = [w.reshape(4 * HEAD_DIM, width) for w in (near, far)]
    mods = modulation(timestep, w_mod, width)

    part_sums = jax.ShapeDtypeStruct((parts, rows, width), BF)
    kept = (
        jax.ShapeDtypeStruct((3, frame_rows, HEAD_DIM), BF),
        jax.ShapeDtypeStruct((frame_rows, frame_rows), BF),
    )
    tokens, term, near_primal, near_probs = call(
        near_kernel,
        (
            jax.ShapeDtypeStruct((2 * frame_rows, width), BF),
            jax.ShapeDtypeStruct((frame_rows, width), F32),
        )
        + kept,
        gath,
        near_flat,
        near,
        mods,
        flops=10**9,
        moved=6 * 10**6,
        limit=24,
    )
    sums, far_primal, far_probs = call(
        far_kernel,
        (part_sums,) + kept,
        tokens,
        far_flat,
        far,
        term,
        flops=10**9,
        moved=4 * 10**6,
        limit=24,
    )
    sums = exchange(sums, "part")
    gated, update = call(
        update_kernel,
        (part_sums, jax.ShapeDtypeStruct((rows, width), F32)),
        sums,
        probes,
        mods,
        moved=10**6,
    )
    gated = exchange(gated, "part")
    sums = call(
        adjoint_kernel,
        part_sums,
        gated,
        near_flat,
        near,
        near_primal,
        near_probs,
        far_flat,
        far,
        far_primal,
        far_probs,
        flops=2 * 10**9,
        moved=5 * 10**6,
        limit=24,
    )
    sums = exchange(sums, "part")
    pairs = jax.ShapeDtypeStruct((chips, rows // chips, width), BF)
    own_rows = jax.ShapeDtypeStruct((rows, width), F32)
    pulled, lost = call(
        pulled_kernel, (pairs, own_rows), sums, update, noisy, mods, moved=10**6
    )
    mine = exchange(pulled, "z")
    other = lax.ppermute(mine, "core", [(i, i ^ 1) for i in range(cores)])
    high = probe_count * probe_count // LANES

    def blocks_of(count):
        return jax.ShapeDtypeStruct((count, high, LANES), F32)

    grams, every = call(
        functools.partial(gram_kernel, 1.0 / float(seq_count * rows * width)),
        (
            blocks_of(seq_count),
            jax.ShapeDtypeStruct((probe_count, rows // chips, width), BF),
        ),
        mine,
        other,
        moved=10**5,
    )
    grams = exchange(grams, SEQ)
    grams = call(total_kernel, blocks_of(chips), grams, moved=10**5)
    factor, solved, rest = call(
        solve_kernel,
        (jax.ShapeDtypeStruct((probe_count, probe_count), F32), pairs, own_rows),
        exchange(grams, "z"),
        every,
        lost,
        moved=3 * 10**5,
    )
    basis = call(
        basis_kernel,
        jax.ShapeDtypeStruct((1, rows, width), F32),
        exchange(solved, "z"),
        rest,
        moved=3 * 10**5,
    )
    return basis, factor


def solution(mesh):
    split = Mesh(
        mesh.devices.reshape(
            mesh.shape["probe"] // 2, 2, FRAMES, mesh.shape["seq"] // FRAMES
        ),
        PROBE + SEQ,
    )
    placed = (P(SEQ, None), P(PROBE, SEQ, None), P(None, SEQ), P(SEQ, None), P(), P())
    return jax.shard_map(
        shards,
        mesh=split,
        in_specs=placed,
        out_specs=(P(PROBE, SEQ, None), P()),
        check_vma=False,
    )
```

```python
import functools
import math

import jax
import jax.numpy as jnp
from jax import lax
from jax.experimental import pallas as pl
from jax.experimental.pallas import tpu as pltpu
from jax.sharding import Mesh
from jax.sharding import PartitionSpec as P

HEAD_DIM = 72
LANES = 128
FRAMES = 2
SEQ = ("frame", "part")
PROBE = ("z", "core")
MIB = 1024 * 1024
STEP = 4
NT = (((1,), (1,)), ((), ()))
NN = (((1,), (0,)), ((), ()))
BF = jnp.bfloat16
F32 = jnp.float32


def mm(a, b, dims=NN):
    return lax.dot_general(a, b, dims, preferred_element_type=F32)


def exact(a, b, dims=NN):
    return lax.dot_general(
        a, b, dims, precision=lax.Precision.HIGHEST, preferred_element_type=F32
    )


def eye(n):
    row = lax.broadcasted_iota(jnp.int32, (n, n), 0)
    col = lax.broadcasted_iota(jnp.int32, (n, n), 1)
    return jnp.where(row == col, 1.0, 0.0)


def flip(a):
    return mm(eye(a.shape[1]).astype(BF), a, NT).astype(BF)


def modulation(timestep, w_mod, feat_width):
    half_dim = w_mod.shape[0] // 2
    freq_index = jnp.arange(half_dim, dtype=jnp.float32)
    frequency = jnp.exp(-math.log(10000.0) * freq_index / half_dim)
    angles = timestep[0].astype(jnp.float32) * frequency
    embedding = jnp.concatenate([jnp.cos(angles), jnp.sin(angles)])
    modulated = jnp.dot(
        jax.nn.silu(embedding)[None, :], w_mod.astype(jnp.float32), precision=lax.Precision.HIGHEST
    )
    return modulated.reshape(3, feat_width)


def normalize(values_f):
    centered = values_f - jnp.mean(values_f, axis=-1, keepdims=True)
    inverse = 1.0 / jnp.sqrt(jnp.mean(centered * centered, axis=-1, keepdims=True) + 1e-06)
    return centered * inverse, inverse


def norm_tangent(field, normed, inverse):
    mean_part = jnp.mean(field, axis=-1, keepdims=True)
    along = jnp.mean(field * normed, axis=-1, keepdims=True)
    return (field - mean_part - normed * along) * inverse


def fetch(pairs, sems):
    copies = [pltpu.make_async_copy(a, b, sems.at[i]) for i, (a, b) in enumerate(pairs)]
    for copy in copies:
        copy.start()
    return copies


def copies_kernel(noisy, probe, out, staged, sems):
    count = out.shape[0]
    for copy in fetch([(noisy, staged.at[0]), (probe.at[0], staged.at[1])], sems):
        copy.wait()
    for copy in fetch([(staged, out.at[j]) for j in range(count)], sems.at[pl.ds(2, count)]):
        copy.wait()


def thirds(value):
    return [value[:, i * HEAD_DIM : (i + 1) * HEAD_DIM].astype(BF) for i in range(3)]


def head_forward(tokens, w_in, primal, probs):
    c = HEAD_DIM ** (-0.5)
    count = tokens.shape[0] // 2
    projected = mm(tokens[...], w_in[...], NT)
    q, k, v = thirds(projected[:count])
    dq, dk, dv = thirds(projected[count:])
    scores = mm(q, k, NT) * c
    expon = jnp.exp(scores - jnp.max(scores, axis=-1, keepdims=True))
    p = (expon * (1.0 / jnp.sum(expon, axis=-1, keepdims=True))).astype(BF)
    d_scores = (mm(dq, k, NT) + mm(q, dk, NT)) * c
    mixed = p.astype(F32) * d_scores
    row_sum = jnp.sum(mixed, axis=-1, keepdims=True)
    out = mm(mixed.astype(BF), v) + mm(p, dv) - row_sum * mm(p, v)
    probs[...] = p
    for i, value in enumerate((q, k, v)):
        primal[i] = value
    return out.astype(BF)


def near_kernel(gath, w_in, w_out, mods, tokens, term, primal, probs):
    blocks, _, rows, _ = gath.shape
    scale = 1.0 + mods[1:2, :]
    shift = mods[0:1, :]
    for i in range(blocks):
        normed, inverse = normalize(gath[i, 0].astype(F32))
        tokens[pl.ds(i * rows, rows), :] = (normed * scale + shift).astype(BF)
        field = norm_tangent(gath[i, 1].astype(F32), normed, inverse)
        tokens[pl.ds((blocks + i) * rows, rows), :] = (field * scale).astype(BF)
    term[...] = mm(head_forward(tokens, w_in, primal, probs), w_out[...])


def far_kernel(tokens, w_in, out, primal, probs):
    out[...] = head_forward(tokens, w_in, primal, probs)


def sum_kernel(term, out, w_out, parts):
    total = term[...] + mm(out[...], w_out[...])
    parts[...] = total.astype(BF).reshape(parts.shape)


def update_kernel(parts, probe, mods, gated, update):
    total = parts[0].astype(F32)
    for j in range(1, parts.shape[0]):
        total = total + parts[j].astype(F32)
    gate = mods[2:3, :]
    fresh = probe[0].astype(F32) + gate * total
    update[...] = fresh
    value = (gate * fresh).astype(BF)
    for j in range(gated.shape[0]):
        gated[j] = value


def adjoint_kernel(
    gated, near_in, near_out, near_primal, near_probs, far_in, far_out, far_primal, far_probs, parts
):
    c = HEAD_DIM ** (-0.5)
    blocks, rows, width = gated.shape
    whole = gated[...].reshape(blocks * rows, width)
    total = None
    for w_in, w_out, primal, probs in (
        (near_in, near_out, near_primal, near_probs),
        (far_in, far_out, far_primal, far_probs),
    ):
        co = mm(whole, w_out[...], NT).astype(BF)
        q, k, v = primal[0], primal[1], primal[2]
        p = probs[...]
        p_float = p.astype(F32)
        d_probs = mm(co, v, NT)
        row_dot = jnp.sum(p_float * d_probs, axis=-1, keepdims=True)
        scaled = (p_float * (d_probs - row_dot) * c).astype(BF)
        grads = (mm(scaled, k), mm(flip(scaled), q), mm(flip(p), co))
        grads = jnp.concatenate(grads, axis=1).astype(BF)
        term = mm(grads, w_in[...])
        total = term if total is None else total + term
    parts[...] = total.astype(BF).reshape(parts.shape)


def pulled_kernel(parts, update, noisy, mods, pulled, lost):
    total = parts[0].astype(F32)
    for j in range(1, parts.shape[0]):
        total = total + parts[j].astype(F32)
    normed, inverse = normalize(noisy[...].astype(F32))
    value = update[...] + norm_tangent((1.0 + mods[1:2, :]) * total, normed, inverse)
    rounded = value.astype(BF)
    lost[...] = value - rounded.astype(F32)
    pairs, each, _ = pulled.shape
    for i in range(pairs):
        pulled[i] = value[i * each : (i + 1) * each].astype(BF)


def gram_kernel(scale, mine, other, copies, rows):
    first = lax.axis_index("core") == 0
    for i in range(mine.shape[0]):
        rows[2 * i] = jnp.where(first, mine[i], other[i])
        rows[2 * i + 1] = jnp.where(first, other[i], mine[i])
    each = [rows[:, t, :] for t in range(rows.shape[1])]
    gram = sum(mm(row, row, NT) for row in each) * scale
    n = gram.shape[0]
    width = LANES // n
    high = n // width
    packed = jnp.concatenate([gram[i * high : (i + 1) * high] for i in range(width)], axis=1)
    for j in range(copies.shape[0]):
        copies[j] = packed


def tree_sum(terms):
    while len(terms) > 1:
        terms = [terms[i] + terms[i + 1] for i in range(0, len(terms), 2)]
    return terms[0]


def total_kernel(arrived, copies):
    total = tree_sum([arrived[j] for j in range(arrived.shape[0])])
    for j in range(copies.shape[0]):
        copies[j] = total


def picked(n, core):
    row = lax.broadcasted_iota(jnp.int32, (n // 2, n), 0)
    col = lax.broadcasted_iota(jnp.int32, (n // 2, n), 1)
    return jnp.where(col == 2 * row + core, 1.0, 0.0)


def solve_kernel(arrived, rows, lost, factor, solved, rest):
    packed = tree_sum([arrived[j] for j in range(arrived.shape[0])])
    n = factor.shape[0]
    width = LANES // n
    a = jnp.concatenate([packed[:, i * n : (i + 1) * n] for i in range(width)], axis=0)
    both = jnp.concatenate([a, eye(n)], axis=1)
    row = lax.broadcasted_iota(jnp.int32, both.shape, 0)
    col = lax.broadcasted_iota(jnp.int32, both.shape, 1)
    wide = (1, both.shape[1])
    for j in range(0, n, STEP):
        span = range(STEP)
        tops = [both[j + i : j + i + 1, :] for i in span]
        sides = [jnp.broadcast_to(both[:, j + i : j + i + 1], both.shape) for i in span]
        corner = [
            [jnp.broadcast_to(tops[i][:, j + k : j + k + 1], wide) for k in span] for i in span
        ]
        change = jnp.zeros_like(both)
        for i in span:
            inverse = 1.0 / corner[i][i]
            for k in range(i + 1, STEP):
                ratio = corner[i][k] * inverse
                tops[k] = tops[k] - ratio * tops[i]
                sides[k] = sides[k] - ratio * sides[i]
                for m in range(k, STEP):
                    corner[k][m] = corner[k][m] - ratio * corner[i][m]
            change = change + sides[i] * (tops[i] * inverse)
        below = both - jnp.where(row >= j + STEP, change, 0.0)
        for i in span:
            below = jnp.where(row == j + i, tops[i], below)
        both = below
    pivots = jnp.sum(jnp.where(row == col, both, 0.0), axis=1, keepdims=True)
    both = both / jnp.sqrt(pivots)
    factor[...] = jnp.where(col >= row, both, 0.0)[:, :n]
    core = lax.axis_index("core")
    own = lax.axis_index("z") * 2 + core
    square = jnp.where((row == own) & (col == own), both, 0.0)
    pivot = jnp.sum(jnp.sum(square, axis=0, keepdims=True), axis=1, keepdims=True)
    rest[...] = lost[...] * (1.0 / pivot)
    remains = both[:, n:]
    choice = picked(n, core).astype(BF)
    pieces = []
    for _ in range(3):
        piece = remains.astype(BF)
        pieces.append(mm(choice, piece))
        remains = remains - piece.astype(F32)
    pieces = jnp.concatenate(pieces, axis=0).astype(BF)
    for t in range(rows.shape[1]):
        product = mm(pieces, rows[:, t, :])
        high, middle, low = [product[i * n // 2 : (i + 1) * n // 2] for i in range(3)]
        solved[:, t, :] = (high + (middle + low)).astype(BF)


def basis_kernel(pairs, rest, basis):
    count, each, _ = pairs.shape
    for i in range(count):
        at = slice(i * each, (i + 1) * each)
        basis[0, at, :] = pairs[i].astype(F32) + rest[at, :]


HBM = pl.BlockSpec(memory_space=pl.ANY)
LOCAL = pl.BlockSpec(memory_space=pltpu.VMEM)


def call(
    kernel, out_shape, *args, where=None, out_specs=None, scratch=(), flops=0, moved=0, limit=8
):
    return pl.pallas_call(
        kernel,
        out_shape=out_shape,
        in_specs=where or [LOCAL] * len(args),
        out_specs=out_specs or jax.tree.map(lambda _: LOCAL, out_shape),
        scratch_shapes=list(scratch),
        compiler_params=pltpu.CompilerParams(vmem_limit_bytes=limit * MIB),
        cost_estimate=pl.CostEstimate(flops=flops, bytes_accessed=moved, transcendentals=0),
    )(*args)


def exchange(blocks, axis):
    return lax.all_to_all(blocks, axis, split_axis=0, concat_axis=0, tiled=True)


def shards(noisy, probes, w_qkv, w_out, w_mod, timestep):
    rows, width = noisy.shape
    parts, frames, cores, chips = [lax.axis_size(n) for n in ("part", "frame", "core", "z")]
    seq_count = parts * frames
    probe_count = cores * chips
    frame_rows = parts * rows

    outgoing = call(
        copies_kernel,
        jax.ShapeDtypeStruct((parts, 2, rows, width), BF),
        noisy,
        probes,
        where=[HBM, HBM],
        out_specs=HBM,
        scratch=(
            pltpu.VMEM((2, rows, width), BF),
            pltpu.SemaphoreType.DMA((2 + parts,)),
        ),
        moved=2 * 10**6,
        limit=60,
    )
    outgoing, w_in, w_out = lax.optimization_barrier((outgoing, w_qkv.T, w_out))
    gath = exchange(outgoing, "part")
    half = seq_count - seq_count // 4
    partner = [(i, i ^ half) for i in range(seq_count)]
    far_in = lax.ppermute(w_in, SEQ, partner)
    far_out = lax.ppermute(w_out, SEQ, partner)
    mods = modulation(timestep, w_mod, width)

    part_sums = jax.ShapeDtypeStruct((parts, rows, width), BF)
    kept = (
        jax.ShapeDtypeStruct((3, frame_rows, HEAD_DIM), BF),
        jax.ShapeDtypeStruct((frame_rows, frame_rows), BF),
    )
    tokens, term, near_primal, near_probs = call(
        near_kernel,
        (
            jax.ShapeDtypeStruct((2 * frame_rows, width), BF),
            jax.ShapeDtypeStruct((frame_rows, width), F32),
        )
        + kept,
        gath,
        w_in,
        w_out,
        mods,
        flops=10**9,
        moved=6 * 10**6,
        limit=24,
    )
    out, far_primal, far_probs = call(
        far_kernel,
        (jax.ShapeDtypeStruct((frame_rows, HEAD_DIM), BF),) + kept,
        tokens,
        far_in,
        flops=10**9,
        moved=4 * 10**6,
        limit=24,
    )
    sums = call(sum_kernel, part_sums, term, out, far_out, flops=10**8, moved=10**6)
    sums = exchange(sums, "part")
    gated, update = call(
        update_kernel,
        (part_sums, jax.ShapeDtypeStruct((rows, width), F32)),
        sums,
        probes,
        mods,
        moved=10**6,
    )
    gated = exchange(gated, "part")
    sums = call(
        adjoint_kernel,
        part_sums,
        gated,
        w_in,
        w_out,
        near_primal,
        near_probs,
        far_in,
        far_out,
        far_primal,
        far_probs,
        flops=2 * 10**9,
        moved=5 * 10**6,
        limit=24,
    )
    sums = exchange(sums, "part")
    pairs = jax.ShapeDtypeStruct((chips, rows // chips, width), BF)
    own_rows = jax.ShapeDtypeStruct((rows, width), F32)
    pulled, lost = call(
        pulled_kernel, (pairs, own_rows), sums, update, noisy, mods, moved=10**6
    )
    mine = exchange(pulled, "z")
    other = lax.ppermute(mine, "core", [(i, i ^ 1) for i in range(cores)])
    high = probe_count * probe_count // LANES

    def blocks_of(count):
        return jax.ShapeDtypeStruct((count, high, LANES), F32)

    grams, every = call(
        functools.partial(gram_kernel, 1.0 / float(seq_count * rows * width)),
        (
            blocks_of(seq_count),
            jax.ShapeDtypeStruct((probe_count, rows // chips, width), BF),
        ),
        mine,
        other,
        moved=10**5,
    )
    grams = exchange(grams, SEQ)
    grams = call(total_kernel, blocks_of(chips), grams, moved=10**5)
    factor, solved, rest = call(
        solve_kernel,
        (jax.ShapeDtypeStruct((probe_count, probe_count), F32), pairs, own_rows),
        exchange(grams, "z"),
        every,
        lost,
        moved=3 * 10**5,
    )
    basis = call(
        basis_kernel,
        jax.ShapeDtypeStruct((1, rows, width), F32),
        exchange(solved, "z"),
        rest,
        moved=3 * 10**5,
    )
    return basis, factor


def solution(mesh):
    split = Mesh(
        mesh.devices.reshape(
            mesh.shape["probe"] // 2, 2, FRAMES, mesh.shape["seq"] // FRAMES
        ),
        PROBE + SEQ,
    )
    placed = (P(SEQ, None), P(PROBE, SEQ, None), P(None, SEQ), P(SEQ, None), P(), P())
    return jax.shard_map(
        shards,
        mesh=split,
        in_specs=placed,
        out_specs=(P(PROBE, SEQ, None), P()),
        check_vma=False,
    )
```

```python
import functools
import math

import jax
import jax.numpy as jnp
from jax import lax
from jax.experimental import pallas as pl
from jax.experimental.pallas import tpu as pltpu
from jax.sharding import Mesh
from jax.sharding import PartitionSpec as P

HEAD_DIM = 72
LANES = 128
FRAMES = 2
SEQ = ("frame", "part")
PROBE = ("z", "core")
MIB = 1024 * 1024
STEP = 4
NT = (((1,), (1,)), ((), ()))
NN = (((1,), (0,)), ((), ()))
BF = jnp.bfloat16
F32 = jnp.float32


def mm(a, b, dims=NN):
    return lax.dot_general(a, b, dims, preferred_element_type=F32)


def exact(a, b, dims=NN):
    return lax.dot_general(
        a, b, dims, precision=lax.Precision.HIGHEST, preferred_element_type=F32
    )


def eye(n):
    row = lax.broadcasted_iota(jnp.int32, (n, n), 0)
    col = lax.broadcasted_iota(jnp.int32, (n, n), 1)
    return jnp.where(row == col, 1.0, 0.0)


def flip(a):
    return mm(eye(a.shape[1]).astype(BF), a, NT).astype(BF)


def modulation(timestep, w_mod, feat_width):
    half_dim = w_mod.shape[0] // 2
    freq_index = jnp.arange(half_dim, dtype=jnp.float32)
    frequency = jnp.exp(-math.log(10000.0) * freq_index / half_dim)
    angles = timestep[0].astype(jnp.float32) * frequency
    rest = jax.nn.silu(jnp.concatenate([jnp.cos(angles), jnp.sin(angles)]))
    pieces = []
    for _ in range(3):
        pieces.append(lax.reduce_precision(rest, 8, 7))
        rest = rest - pieces[-1]
    rows = jnp.pad(jnp.stack(pieces), ((0, 13), (0, 0))).astype(BF)
    return jnp.sum(mm(rows, w_mod), axis=0).reshape(3, feat_width)


def normalize(values_f):
    centered = values_f - jnp.mean(values_f, axis=-1, keepdims=True)
    inverse = 1.0 / jnp.sqrt(jnp.mean(centered * centered, axis=-1, keepdims=True) + 1e-06)
    return centered * inverse, inverse


def norm_tangent(field, normed, inverse):
    mean_part = jnp.mean(field, axis=-1, keepdims=True)
    along = jnp.mean(field * normed, axis=-1, keepdims=True)
    return (field - mean_part - normed * along) * inverse


def fetch(pairs, sems):
    copies = [pltpu.make_async_copy(a, b, sems.at[i]) for i, (a, b) in enumerate(pairs)]
    for copy in copies:
        copy.start()
    return copies


def copies_kernel(noisy, probe, out, staged, sems):
    count = out.shape[0]
    for copy in fetch([(noisy, staged.at[0]), (probe.at[0], staged.at[1])], sems):
        copy.wait()
    for copy in fetch([(staged, out.at[j]) for j in range(count)], sems.at[pl.ds(2, count)]):
        copy.wait()


def thirds(value):
    return [value[:, i * HEAD_DIM : (i + 1) * HEAD_DIM].astype(BF) for i in range(3)]


def head_forward(tokens, w_in, primal, probs):
    c = HEAD_DIM ** (-0.5)
    count = tokens.shape[0] // 2
    projected = mm(tokens[...], w_in[...], NT)
    q, k, v = thirds(projected[:count])
    dq, dk, dv = thirds(projected[count:])
    scores = mm(q, k, NT) * c
    expon = jnp.exp(scores - jnp.max(scores, axis=-1, keepdims=True))
    p = (expon * (1.0 / jnp.sum(expon, axis=-1, keepdims=True))).astype(BF)
    d_scores = (mm(dq, k, NT) + mm(q, dk, NT)) * c
    mixed = p.astype(F32) * d_scores
    row_sum = jnp.sum(mixed, axis=-1, keepdims=True)
    out = mm(mixed.astype(BF), v) + mm(p, dv) - row_sum * mm(p, v)
    probs[...] = p
    for i, value in enumerate((q, k, v)):
        primal[i] = value
    return out.astype(BF)


def near_kernel(gath, w_in, w_out, mods, tokens, term, primal, probs):
    blocks, _, rows, _ = gath.shape
    scale = 1.0 + mods[1:2, :]
    shift = mods[0:1, :]
    for i in range(blocks):
        normed, inverse = normalize(gath[i, 0].astype(F32))
        tokens[pl.ds(i * rows, rows), :] = (normed * scale + shift).astype(BF)
        field = norm_tangent(gath[i, 1].astype(F32), normed, inverse)
        tokens[pl.ds((blocks + i) * rows, rows), :] = (field * scale).astype(BF)
    term[...] = mm(head_forward(tokens, w_in, primal, probs), w_out[...])


def far_kernel(tokens, w_in, out, primal, probs):
    out[...] = head_forward(tokens, w_in, primal, probs)


def sum_kernel(term, out, w_out, parts):
    total = term[...] + mm(out[...], w_out[...])
    parts[...] = total.astype(BF).reshape(parts.shape)


def update_kernel(parts, probe, mods, gated, update):
    total = parts[0].astype(F32)
    for j in range(1, parts.shape[0]):
        total = total + parts[j].astype(F32)
    gate = mods[2:3, :]
    fresh = probe[0].astype(F32) + gate * total
    update[...] = fresh
    value = (gate * fresh).astype(BF)
    for j in range(gated.shape[0]):
        gated[j] = value


def adjoint_kernel(
    gated, near_in, near_out, near_primal, near_probs, far_in, far_out, far_primal, far_probs, parts
):
    c = HEAD_DIM ** (-0.5)
    blocks, rows, width = gated.shape
    whole = gated[...].reshape(blocks * rows, width)
    total = None
    for w_in, w_out, primal, probs in (
        (near_in, near_out, near_primal, near_probs),
        (far_in, far_out, far_primal, far_probs),
    ):
        co = mm(whole, w_out[...], NT).astype(BF)
        q, k, v = primal[0], primal[1], primal[2]
        p = probs[...]
        p_float = p.astype(F32)
        d_probs = mm(co, v, NT)
        row_dot = jnp.sum(p_float * d_probs, axis=-1, keepdims=True)
        scaled = (p_float * (d_probs - row_dot) * c).astype(BF)
        grads = (mm(scaled, k), mm(flip(scaled), q), mm(flip(p), co))
        grads = jnp.concatenate(grads, axis=1).astype(BF)
        term = mm(grads, w_in[...])
        total = term if total is None else total + term
    parts[...] = total.astype(BF).reshape(parts.shape)


def pulled_kernel(parts, update, noisy, mods, pulled, lost):
    total = parts[0].astype(F32)
    for j in range(1, parts.shape[0]):
        total = total + parts[j].astype(F32)
    normed, inverse = normalize(noisy[...].astype(F32))
    value = update[...] + norm_tangent((1.0 + mods[1:2, :]) * total, normed, inverse)
    rounded = value.astype(BF)
    lost[...] = value - rounded.astype(F32)
    pairs, each, _ = pulled.shape
    for i in range(pairs):
        pulled[i] = value[i * each : (i + 1) * each].astype(BF)


def gram_kernel(scale, mine, other, copies, rows):
    first = lax.axis_index("core") == 0
    for i in range(mine.shape[0]):
        rows[2 * i] = jnp.where(first, mine[i], other[i])
        rows[2 * i + 1] = jnp.where(first, other[i], mine[i])
    each = [rows[:, t, :] for t in range(rows.shape[1])]
    gram = sum(mm(row, row, NT) for row in each) * scale
    n = gram.shape[0]
    width = LANES // n
    high = n // width
    packed = jnp.concatenate([gram[i * high : (i + 1) * high] for i in range(width)], axis=1)
    for j in range(copies.shape[0]):
        copies[j] = packed


def tree_sum(terms):
    while len(terms) > 1:
        terms = [terms[i] + terms[i + 1] for i in range(0, len(terms), 2)]
    return terms[0]


def total_kernel(arrived, copies):
    total = tree_sum([arrived[j] for j in range(arrived.shape[0])])
    for j in range(copies.shape[0]):
        copies[j] = total


def picked(n, core):
    row = lax.broadcasted_iota(jnp.int32, (n // 2, n), 0)
    col = lax.broadcasted_iota(jnp.int32, (n // 2, n), 1)
    return jnp.where(col == 2 * row + core, 1.0, 0.0)


def solve_kernel(arrived, rows, lost, factor, solved, rest):
    packed = tree_sum([arrived[j] for j in range(arrived.shape[0])])
    n = factor.shape[0]
    width = LANES // n
    a = jnp.concatenate([packed[:, i * n : (i + 1) * n] for i in range(width)], axis=0)
    both = jnp.concatenate([a, eye(n)], axis=1)
    row = lax.broadcasted_iota(jnp.int32, both.shape, 0)
    col = lax.broadcasted_iota(jnp.int32, both.shape, 1)
    wide = (1, both.shape[1])
    for j in range(0, n, STEP):
        span = range(STEP)
        tops = [both[j + i : j + i + 1, :] for i in span]
        sides = [jnp.broadcast_to(both[:, j + i : j + i + 1], both.shape) for i in span]
        corner = [
            [jnp.broadcast_to(tops[i][:, j + k : j + k + 1], wide) for k in span] for i in span
        ]
        change = jnp.zeros_like(both)
        for i in span:
            inverse = 1.0 / corner[i][i]
            for k in range(i + 1, STEP):
                ratio = corner[i][k] * inverse
                tops[k] = tops[k] - ratio * tops[i]
                sides[k] = sides[k] - ratio * sides[i]
                for m in range(k, STEP):
                    corner[k][m] = corner[k][m] - ratio * corner[i][m]
            change = change + sides[i] * (tops[i] * inverse)
        below = both - jnp.where(row >= j + STEP, change, 0.0)
        for i in span:
            below = jnp.where(row == j + i, tops[i], below)
        both = below
    pivots = jnp.sum(jnp.where(row == col, both, 0.0), axis=1, keepdims=True)
    both = both / jnp.sqrt(pivots)
    factor[...] = jnp.where(col >= row, both, 0.0)[:, :n]
    core = lax.axis_index("core")
    own = lax.axis_index("z") * 2 + core
    square = jnp.where((row == own) & (col == own), both, 0.0)
    pivot = jnp.sum(jnp.sum(square, axis=0, keepdims=True), axis=1, keepdims=True)
    rest[...] = lost[...] * (1.0 / pivot)
    remains = both[:, n:]
    choice = picked(n, core).astype(BF)
    pieces = []
    for _ in range(3):
        piece = remains.astype(BF)
        pieces.append(mm(choice, piece))
        remains = remains - piece.astype(F32)
    pieces = jnp.concatenate(pieces, axis=0).astype(BF)
    for t in range(rows.shape[1]):
        product = mm(pieces, rows[:, t, :])
        high, middle, low = [product[i * n // 2 : (i + 1) * n // 2] for i in range(3)]
        solved[:, t, :] = (high + (middle + low)).astype(BF)


def basis_kernel(pairs, rest, triangle, basis, factor):
    factor[...] = triangle[...]
    count, each, _ = pairs.shape
    for i in range(count):
        at = slice(i * each, (i + 1) * each)
        basis[0, at, :] = pairs[i].astype(F32) + rest[at, :]


HBM = pl.BlockSpec(memory_space=pl.ANY)
LOCAL = pl.BlockSpec(memory_space=pltpu.VMEM)


def call(
    kernel, out_shape, *args, where=None, out_specs=None, scratch=(), flops=0, moved=0, limit=8
):
    return pl.pallas_call(
        kernel,
        out_shape=out_shape,
        in_specs=where or [LOCAL] * len(args),
        out_specs=out_specs or jax.tree.map(lambda _: LOCAL, out_shape),
        scratch_shapes=list(scratch),
        compiler_params=pltpu.CompilerParams(vmem_limit_bytes=limit * MIB),
        cost_estimate=pl.CostEstimate(flops=flops, bytes_accessed=moved, transcendentals=0),
    )(*args)


def exchange(blocks, axis):
    return lax.all_to_all(blocks, axis, split_axis=0, concat_axis=0, tiled=True)


def shards(noisy, probes, w_qkv, w_out, w_mod, timestep):
    rows, width = noisy.shape
    parts, frames, cores, chips = [lax.axis_size(n) for n in ("part", "frame", "core", "z")]
    seq_count = parts * frames
    probe_count = cores * chips
    frame_rows = parts * rows

    outgoing = call(
        copies_kernel,
        jax.ShapeDtypeStruct((parts, 2, rows, width), BF),
        noisy,
        probes,
        where=[HBM, HBM],
        out_specs=HBM,
        scratch=(
            pltpu.VMEM((2, rows, width), BF),
            pltpu.SemaphoreType.DMA((2 + parts,)),
        ),
        moved=2 * 10**6,
        limit=60,
    )
    outgoing, w_in, w_out = lax.optimization_barrier((outgoing, w_qkv.T, w_out))
    gath = exchange(outgoing, "part")
    half = seq_count - seq_count // 4
    partner = [(i, i ^ half) for i in range(seq_count)]
    far_in = lax.ppermute(w_in, SEQ, partner)
    far_out = lax.ppermute(w_out, SEQ, partner)
    mods = modulation(timestep, w_mod, width)

    part_sums = jax.ShapeDtypeStruct((parts, rows, width), BF)
    kept = (
        jax.ShapeDtypeStruct((3, frame_rows, HEAD_DIM), BF),
        jax.ShapeDtypeStruct((frame_rows, frame_rows), BF),
    )
    tokens, term, near_primal, near_probs = call(
        near_kernel,
        (
            jax.ShapeDtypeStruct((2 * frame_rows, width), BF),
            jax.ShapeDtypeStruct((frame_rows, width), F32),
        )
        + kept,
        gath,
        w_in,
        w_out,
        mods,
        flops=10**9,
        moved=6 * 10**6,
        limit=24,
    )
    out, far_primal, far_probs = call(
        far_kernel,
        (jax.ShapeDtypeStruct((frame_rows, HEAD_DIM), BF),) + kept,
        tokens,
        far_in,
        flops=10**9,
        moved=4 * 10**6,
        limit=24,
    )
    sums = call(sum_kernel, part_sums, term, out, far_out, flops=10**8, moved=10**6)
    sums = exchange(sums, "part")
    gated, update = call(
        update_kernel,
        (part_sums, jax.ShapeDtypeStruct((rows, width), F32)),
        sums,
        probes,
        mods,
        moved=10**6,
    )
    gated = exchange(gated, "part")
    sums = call(
        adjoint_kernel,
        part_sums,
        gated,
        w_in,
        w_out,
        near_primal,
        near_probs,
        far_in,
        far_out,
        far_primal,
        far_probs,
        flops=2 * 10**9,
        moved=5 * 10**6,
        limit=24,
    )
    sums = exchange(sums, "part")
    pairs = jax.ShapeDtypeStruct((chips, rows // chips, width), BF)
    own_rows = jax.ShapeDtypeStruct((rows, width), F32)
    pulled, lost = call(
        pulled_kernel, (pairs, own_rows), sums, update, noisy, mods, moved=10**6
    )
    mine = exchange(pulled, "z")
    other = lax.ppermute(mine, "core", [(i, i ^ 1) for i in range(cores)])
    high = probe_count * probe_count // LANES

    def blocks_of(count):
        return jax.ShapeDtypeStruct((count, high, LANES), F32)

    grams, every = call(
        functools.partial(gram_kernel, 1.0 / float(seq_count * rows * width)),
        (
            blocks_of(seq_count),
            jax.ShapeDtypeStruct((probe_count, rows // chips, width), BF),
        ),
        mine,
        other,
        moved=10**5,
    )
    grams = exchange(grams, SEQ)
    grams = call(total_kernel, blocks_of(chips), grams, moved=10**5)
    square = jax.ShapeDtypeStruct((probe_count, probe_count), F32)
    triangle, solved, rest = call(
        solve_kernel,
        (square, pairs, own_rows),
        exchange(grams, "z"),
        every,
        lost,
        moved=3 * 10**5,
    )
    basis, factor = call(
        basis_kernel,
        (jax.ShapeDtypeStruct((1, rows, width), F32), square),
        exchange(solved, "z"),
        rest,
        triangle,
        moved=3 * 10**5,
    )
    return basis, factor


def solution(mesh):
    split = Mesh(
        mesh.devices.reshape(
            mesh.shape["probe"] // 2, 2, FRAMES, mesh.shape["seq"] // FRAMES
        ),
        PROBE + SEQ,
    )
    placed = (P(SEQ, None), P(PROBE, SEQ, None), P(None, SEQ), P(SEQ, None), P(), P())
    return jax.shard_map(
        shards,
        mesh=split,
        in_specs=placed,
        out_specs=(P(PROBE, SEQ, None), P()),
        check_vma=False,
    )
```

```python
import functools
import math

import jax
import jax.numpy as jnp
from jax import lax
from jax.experimental import pallas as pl
from jax.experimental.pallas import tpu as pltpu
from jax.sharding import Mesh
from jax.sharding import PartitionSpec as P

HEAD_DIM = 72
LANES = 128
FRAMES = 2
SEQ = ("frame", "part")
PROBE = ("z", "core")
MIB = 1024 * 1024
STEP = 4
NT = (((1,), (1,)), ((), ()))
NN = (((1,), (0,)), ((), ()))
BF = jnp.bfloat16
F32 = jnp.float32


def mm(a, b, dims=NN):
    return lax.dot_general(a, b, dims, preferred_element_type=F32)


def exact(a, b, dims=NN):
    return lax.dot_general(
        a, b, dims, precision=lax.Precision.HIGHEST, preferred_element_type=F32
    )


def eye(n):
    row = lax.broadcasted_iota(jnp.int32, (n, n), 0)
    col = lax.broadcasted_iota(jnp.int32, (n, n), 1)
    return jnp.where(row == col, 1.0, 0.0)


def flip(a):
    return mm(eye(a.shape[1]).astype(BF), a, NT).astype(BF)


def embedding_rows(timestep, freq_dim):
    half_dim = freq_dim // 2
    freq_index = jnp.arange(half_dim, dtype=jnp.float32)
    frequency = jnp.exp(-math.log(10000.0) * freq_index / half_dim)
    angles = timestep[0].astype(jnp.float32) * frequency
    rest = jax.nn.silu(jnp.concatenate([jnp.cos(angles), jnp.sin(angles)]))
    pieces = []
    for _ in range(3):
        pieces.append(lax.reduce_precision(rest, 8, 7))
        rest = rest - pieces[-1]
    return jnp.pad(jnp.stack(pieces), ((0, 13), (0, 0))).astype(BF)


def modulation_kernel(embedding, w_mod, mods, staged, sems):
    width = mods.shape[1]
    spans = [pl.ds(i * width, width) for i in range(3)]
    copies = fetch([(w_mod.at[:, at], staged.at[:, at]) for at in spans], sems)
    for i, at in enumerate(spans):
        copies[i].wait()
        mods[i : i + 1, :] = jnp.sum(mm(embedding[...], staged[:, at]), axis=0, keepdims=True)


def normalize(values_f):
    centered = values_f - jnp.mean(values_f, axis=-1, keepdims=True)
    inverse = 1.0 / jnp.sqrt(jnp.mean(centered * centered, axis=-1, keepdims=True) + 1e-06)
    return centered * inverse, inverse


def norm_tangent(field, normed, inverse):
    mean_part = jnp.mean(field, axis=-1, keepdims=True)
    along = jnp.mean(field * normed, axis=-1, keepdims=True)
    return (field - mean_part - normed * along) * inverse


def fetch(pairs, sems):
    copies = [pltpu.make_async_copy(a, b, sems.at[i]) for i, (a, b) in enumerate(pairs)]
    for copy in copies:
        copy.start()
    return copies


def copies_kernel(noisy, probe, out, staged, sems):
    count = out.shape[0]
    for copy in fetch([(noisy, staged.at[0]), (probe.at[0], staged.at[1])], sems):
        copy.wait()
    for copy in fetch([(staged, out.at[j]) for j in range(count)], sems.at[pl.ds(2, count)]):
        copy.wait()


def thirds(value):
    return [value[:, i * HEAD_DIM : (i + 1) * HEAD_DIM].astype(BF) for i in range(3)]


def head_forward(tokens, w_in, primal, probs):
    c = HEAD_DIM ** (-0.5)
    count = tokens.shape[0] // 2
    projected = mm(tokens[...], w_in[...], NT)
    q, k, v = thirds(projected[:count])
    dq, dk, dv = thirds(projected[count:])
    scores = mm(q, k, NT) * c
    expon = jnp.exp(scores - jnp.max(scores, axis=-1, keepdims=True))
    p = (expon * (1.0 / jnp.sum(expon, axis=-1, keepdims=True))).astype(BF)
    d_scores = (mm(dq, k, NT) + mm(q, dk, NT)) * c
    mixed = p.astype(F32) * d_scores
    row_sum = jnp.sum(mixed, axis=-1, keepdims=True)
    out = mm(mixed.astype(BF), v) + mm(p, dv) - row_sum * mm(p, v)
    probs[...] = p
    for i, value in enumerate((q, k, v)):
        primal[i] = value
    return out.astype(BF)


def near_kernel(gath, w_in, w_out, mods, tokens, term, primal, probs):
    blocks, _, rows, _ = gath.shape
    scale = 1.0 + mods[1:2, :]
    shift = mods[0:1, :]
    for i in range(blocks):
        normed, inverse = normalize(gath[i, 0].astype(F32))
        tokens[pl.ds(i * rows, rows), :] = (normed * scale + shift).astype(BF)
        field = norm_tangent(gath[i, 1].astype(F32), normed, inverse)
        tokens[pl.ds((blocks + i) * rows, rows), :] = (field * scale).astype(BF)
    term[...] = mm(head_forward(tokens, w_in, primal, probs), w_out[...])


def far_kernel(tokens, w_in, out, primal, probs):
    out[...] = head_forward(tokens, w_in, primal, probs)


def sum_kernel(term, out, w_out, parts):
    total = term[...] + mm(out[...], w_out[...])
    parts[...] = total.astype(BF).reshape(parts.shape)


def update_kernel(parts, probe, mods, gated, update):
    total = parts[0].astype(F32)
    for j in range(1, parts.shape[0]):
        total = total + parts[j].astype(F32)
    gate = mods[2:3, :]
    fresh = probe[0].astype(F32) + gate * total
    update[...] = fresh
    value = (gate * fresh).astype(BF)
    for j in range(gated.shape[0]):
        gated[j] = value


def adjoint_kernel(
    gated, near_in, near_out, near_primal, near_probs, far_in, far_out, far_primal, far_probs, parts
):
    c = HEAD_DIM ** (-0.5)
    blocks, rows, width = gated.shape
    whole = gated[...].reshape(blocks * rows, width)
    total = None
    for w_in, w_out, primal, probs in (
        (near_in, near_out, near_primal, near_probs),
        (far_in, far_out, far_primal, far_probs),
    ):
        co = mm(whole, w_out[...], NT).astype(BF)
        q, k, v = primal[0], primal[1], primal[2]
        p = probs[...]
        p_float = p.astype(F32)
        d_probs = mm(co, v, NT)
        row_dot = jnp.sum(p_float * d_probs, axis=-1, keepdims=True)
        scaled = (p_float * (d_probs - row_dot) * c).astype(BF)
        grads = (mm(scaled, k), mm(flip(scaled), q), mm(flip(p), co))
        grads = jnp.concatenate(grads, axis=1).astype(BF)
        term = mm(grads, w_in[...])
        total = term if total is None else total + term
    parts[...] = total.astype(BF).reshape(parts.shape)


def pulled_kernel(parts, update, noisy, mods, pulled, lost):
    total = parts[0].astype(F32)
    for j in range(1, parts.shape[0]):
        total = total + parts[j].astype(F32)
    normed, inverse = normalize(noisy[...].astype(F32))
    value = update[...] + norm_tangent((1.0 + mods[1:2, :]) * total, normed, inverse)
    rounded = value.astype(BF)
    lost[...] = value - rounded.astype(F32)
    pairs, each, _ = pulled.shape
    for i in range(pairs):
        pulled[i] = value[i * each : (i + 1) * each].astype(BF)


def gram_kernel(scale, mine, other, copies, rows):
    first = lax.axis_index("core") == 0
    for i in range(mine.shape[0]):
        rows[2 * i] = jnp.where(first, mine[i], other[i])
        rows[2 * i + 1] = jnp.where(first, other[i], mine[i])
    each = [rows[:, t, :] for t in range(rows.shape[1])]
    gram = sum(mm(row, row, NT) for row in each) * scale
    n = gram.shape[0]
    width = LANES // n
    high = n // width
    packed = jnp.concatenate([gram[i * high : (i + 1) * high] for i in range(width)], axis=1)
    for j in range(copies.shape[0]):
        copies[j] = packed


def tree_sum(terms):
    while len(terms) > 1:
        terms = [terms[i] + terms[i + 1] for i in range(0, len(terms), 2)]
    return terms[0]


def total_kernel(arrived, copies):
    total = tree_sum([arrived[j] for j in range(arrived.shape[0])])
    for j in range(copies.shape[0]):
        copies[j] = total


def picked(n, core):
    row = lax.broadcasted_iota(jnp.int32, (n // 2, n), 0)
    col = lax.broadcasted_iota(jnp.int32, (n // 2, n), 1)
    return jnp.where(col == 2 * row + core, 1.0, 0.0)


def solve_kernel(arrived, rows, lost, factor, solved, rest):
    packed = tree_sum([arrived[j] for j in range(arrived.shape[0])])
    n = factor.shape[0]
    width = LANES // n
    a = jnp.concatenate([packed[:, i * n : (i + 1) * n] for i in range(width)], axis=0)
    both = jnp.concatenate([a, eye(n)], axis=1)
    row = lax.broadcasted_iota(jnp.int32, both.shape, 0)
    col = lax.broadcasted_iota(jnp.int32, both.shape, 1)
    wide = (1, both.shape[1])
    for j in range(0, n, STEP):
        span = range(STEP)
        tops = [both[j + i : j + i + 1, :] for i in span]
        sides = [jnp.broadcast_to(both[:, j + i : j + i + 1], both.shape) for i in span]
        corner = [
            [jnp.broadcast_to(tops[i][:, j + k : j + k + 1], wide) for k in span] for i in span
        ]
        change = jnp.zeros_like(both)
        for i in span:
            inverse = 1.0 / corner[i][i]
            for k in range(i + 1, STEP):
                ratio = corner[i][k] * inverse
                tops[k] = tops[k] - ratio * tops[i]
                sides[k] = sides[k] - ratio * sides[i]
                for m in range(k, STEP):
                    corner[k][m] = corner[k][m] - ratio * corner[i][m]
            change = change + sides[i] * (tops[i] * inverse)
        below = both - jnp.where(row >= j + STEP, change, 0.0)
        for i in span:
            below = jnp.where(row == j + i, tops[i], below)
        both = below
    pivots = jnp.sum(jnp.where(row == col, both, 0.0), axis=1, keepdims=True)
    both = both / jnp.sqrt(pivots)
    factor[...] = jnp.where(col >= row, both, 0.0)[:, :n]
    core = lax.axis_index("core")
    own = lax.axis_index("z") * 2 + core
    square = jnp.where((row == own) & (col == own), both, 0.0)
    pivot = jnp.sum(jnp.sum(square, axis=0, keepdims=True), axis=1, keepdims=True)
    rest[...] = lost[...] * (1.0 / pivot)
    remains = both[:, n:]
    choice = picked(n, core).astype(BF)
    pieces = []
    for _ in range(3):
        piece = remains.astype(BF)
        pieces.append(mm(choice, piece))
        remains = remains - piece.astype(F32)
    pieces = jnp.concatenate(pieces, axis=0).astype(BF)
    for t in range(rows.shape[1]):
        product = mm(pieces, rows[:, t, :])
        high, middle, low = [product[i * n // 2 : (i + 1) * n // 2] for i in range(3)]
        solved[:, t, :] = (high + (middle + low)).astype(BF)


def basis_kernel(pairs, rest, triangle, basis, factor):
    factor[...] = triangle[...]
    count, each, _ = pairs.shape
    for i in range(count):
        at = slice(i * each, (i + 1) * each)
        basis[0, at, :] = pairs[i].astype(F32) + rest[at, :]


HBM = pl.BlockSpec(memory_space=pl.ANY)
LOCAL = pl.BlockSpec(memory_space=pltpu.VMEM)


def call(
    kernel, out_shape, *args, where=None, out_specs=None, scratch=(), flops=0, moved=0, limit=8
):
    return pl.pallas_call(
        kernel,
        out_shape=out_shape,
        in_specs=where or [LOCAL] * len(args),
        out_specs=out_specs or jax.tree.map(lambda _: LOCAL, out_shape),
        scratch_shapes=list(scratch),
        compiler_params=pltpu.CompilerParams(vmem_limit_bytes=limit * MIB),
        cost_estimate=pl.CostEstimate(flops=flops, bytes_accessed=moved, transcendentals=0),
    )(*args)


def exchange(blocks, axis):
    return lax.all_to_all(blocks, axis, split_axis=0, concat_axis=0, tiled=True)


def shards(noisy, probes, w_qkv, w_out, w_mod, timestep):
    rows, width = noisy.shape
    parts, frames, cores, chips = [lax.axis_size(n) for n in ("part", "frame", "core", "z")]
    seq_count = parts * frames
    probe_count = cores * chips
    frame_rows = parts * rows

    outgoing = call(
        copies_kernel,
        jax.ShapeDtypeStruct((parts, 2, rows, width), BF),
        noisy,
        probes,
        where=[HBM, HBM],
        out_specs=HBM,
        scratch=(
            pltpu.VMEM((2, rows, width), BF),
            pltpu.SemaphoreType.DMA((2 + parts,)),
        ),
        moved=2 * 10**6,
        limit=60,
    )
    outgoing, w_in, w_out = lax.optimization_barrier((outgoing, w_qkv.T, w_out))
    gath = exchange(outgoing, "part")
    half = seq_count - seq_count // 4
    partner = [(i, i ^ half) for i in range(seq_count)]
    far_in = lax.ppermute(w_in, SEQ, partner)
    far_out = lax.ppermute(w_out, SEQ, partner)
    mods = call(
        modulation_kernel,
        jax.ShapeDtypeStruct((3, width), F32),
        embedding_rows(timestep, w_mod.shape[0]),
        w_mod,
        where=[LOCAL, HBM],
        scratch=(pltpu.VMEM(w_mod.shape, BF), pltpu.SemaphoreType.DMA((3,))),
        moved=2 * 10**6,
        limit=59,
    )

    part_sums = jax.ShapeDtypeStruct((parts, rows, width), BF)
    kept = (
        jax.ShapeDtypeStruct((3, frame_rows, HEAD_DIM), BF),
        jax.ShapeDtypeStruct((frame_rows, frame_rows), BF),
    )
    tokens, term, near_primal, near_probs = call(
        near_kernel,
        (
            jax.ShapeDtypeStruct((2 * frame_rows, width), BF),
            jax.ShapeDtypeStruct((frame_rows, width), F32),
        )
        + kept,
        gath,
        w_in,
        w_out,
        mods,
        flops=10**9,
        moved=6 * 10**6,
        limit=24,
    )
    out, far_primal, far_probs = call(
        far_kernel,
        (jax.ShapeDtypeStruct((frame_rows, HEAD_DIM), BF),) + kept,
        tokens,
        far_in,
        flops=10**9,
        moved=4 * 10**6,
        limit=24,
    )
    sums = call(sum_kernel, part_sums, term, out, far_out, flops=10**8, moved=10**6)
    sums = exchange(sums, "part")
    gated, update = call(
        update_kernel,
        (part_sums, jax.ShapeDtypeStruct((rows, width), F32)),
        sums,
        probes,
        mods,
        moved=10**6,
    )
    gated = exchange(gated, "part")
    sums = call(
        adjoint_kernel,
        part_sums,
        gated,
        w_in,
        w_out,
        near_primal,
        near_probs,
        far_in,
        far_out,
        far_primal,
        far_probs,
        flops=2 * 10**9,
        moved=5 * 10**6,
        limit=24,
    )
    sums = exchange(sums, "part")
    pairs = jax.ShapeDtypeStruct((chips, rows // chips, width), BF)
    own_rows = jax.ShapeDtypeStruct((rows, width), F32)
    pulled, lost = call(
        pulled_kernel, (pairs, own_rows), sums, update, noisy, mods, moved=10**6
    )
    mine = exchange(pulled, "z")
    other = lax.ppermute(mine, "core", [(i, i ^ 1) for i in range(cores)])
    high = probe_count * probe_count // LANES

    def blocks_of(count):
        return jax.ShapeDtypeStruct((count, high, LANES), F32)

    grams, every = call(
        functools.partial(gram_kernel, 1.0 / float(seq_count * rows * width)),
        (
            blocks_of(seq_count),
            jax.ShapeDtypeStruct((probe_count, rows // chips, width), BF),
        ),
        mine,
        other,
        moved=10**5,
    )
    grams = exchange(grams, SEQ)
    grams = call(total_kernel, blocks_of(chips), grams, moved=10**5)
    square = jax.ShapeDtypeStruct((probe_count, probe_count), F32)
    triangle, solved, rest = call(
        solve_kernel,
        (square, pairs, own_rows),
        exchange(grams, "z"),
        every,
        lost,
        moved=3 * 10**5,
    )
    basis, factor = call(
        basis_kernel,
        (jax.ShapeDtypeStruct((1, rows, width), F32), square),
        exchange(solved, "z"),
        rest,
        triangle,
        moved=3 * 10**5,
    )
    return basis, factor


def solution(mesh):
    split = Mesh(
        mesh.devices.reshape(
            mesh.shape["probe"] // 2, 2, FRAMES, mesh.shape["seq"] // FRAMES
        ),
        PROBE + SEQ,
    )
    placed = (P(SEQ, None), P(PROBE, SEQ, None), P(None, SEQ), P(SEQ, None), P(), P())
    return jax.shard_map(
        shards,
        mesh=split,
        in_specs=placed,
        out_specs=(P(PROBE, SEQ, None), P()),
        check_vma=False,
    )
```

```python
import functools
import math

import jax
import jax.numpy as jnp
from jax import lax
from jax.experimental import pallas as pl
from jax.experimental.pallas import tpu as pltpu
from jax.sharding import Mesh
from jax.sharding import PartitionSpec as P

HEAD_DIM = 72
LANES = 128
FRAMES = 2
SEQ = ("frame", "part")
PROBE = ("z", "core")
MIB = 1024 * 1024
STEP = 4
NT = (((1,), (1,)), ((), ()))
NN = (((1,), (0,)), ((), ()))
BF = jnp.bfloat16
F32 = jnp.float32


def mm(a, b, dims=NN):
    return lax.dot_general(a, b, dims, preferred_element_type=F32)


def exact(a, b, dims=NN):
    return lax.dot_general(
        a, b, dims, precision=lax.Precision.HIGHEST, preferred_element_type=F32
    )


def eye(n):
    row = lax.broadcasted_iota(jnp.int32, (n, n), 0)
    col = lax.broadcasted_iota(jnp.int32, (n, n), 1)
    return jnp.where(row == col, 1.0, 0.0)


def flip(a):
    return mm(eye(a.shape[1]).astype(BF), a, NT).astype(BF)


def modulation(timestep, w_mod, feat_width):
    half_dim = w_mod.shape[0] // 2
    freq_index = jnp.arange(half_dim, dtype=jnp.float32)
    frequency = jnp.exp(-math.log(10000.0) * freq_index / half_dim)
    angles = timestep[0].astype(jnp.float32) * frequency
    embedding = jnp.concatenate([jnp.cos(angles), jnp.sin(angles)])
    modulated = jnp.dot(
        jax.nn.silu(embedding)[None, :], w_mod.astype(jnp.float32), precision=lax.Precision.HIGHEST
    )
    return modulated.reshape(3, feat_width)


def normalize(values_f):
    centered = values_f - jnp.mean(values_f, axis=-1, keepdims=True)
    inverse = 1.0 / jnp.sqrt(jnp.mean(centered * centered, axis=-1, keepdims=True) + 1e-06)
    return centered * inverse, inverse


def norm_tangent(field, normed, inverse):
    mean_part = jnp.mean(field, axis=-1, keepdims=True)
    along = jnp.mean(field * normed, axis=-1, keepdims=True)
    return (field - mean_part - normed * along) * inverse


def fetch(pairs, sems):
    copies = [pltpu.make_async_copy(a, b, sems.at[i]) for i, (a, b) in enumerate(pairs)]
    for copy in copies:
        copy.start()
    return copies


def copies_kernel(noisy, probe, out, staged, sems):
    count = out.shape[0]
    for copy in fetch([(noisy, staged.at[0]), (probe.at[0], staged.at[1])], sems):
        copy.wait()
    for copy in fetch([(staged, out.at[j]) for j in range(count)], sems.at[pl.ds(2, count)]):
        copy.wait()


def thirds(value):
    return [value[:, i * HEAD_DIM : (i + 1) * HEAD_DIM].astype(BF) for i in range(3)]


def head_forward(tokens, w_in, primal, probs):
    c = HEAD_DIM ** (-0.5)
    count = tokens.shape[0] // 2
    projected = mm(tokens[...], w_in[...], NT)
    q, k, v = thirds(projected[:count])
    dq, dk, dv = thirds(projected[count:])
    scores = mm(q, k, NT) * c
    expon = jnp.exp(scores - jnp.max(scores, axis=-1, keepdims=True))
    p = (expon * (1.0 / jnp.sum(expon, axis=-1, keepdims=True))).astype(BF)
    d_scores = (mm(dq, k, NT) + mm(q, dk, NT)) * c
    mixed = p.astype(F32) * d_scores
    row_sum = jnp.sum(mixed, axis=-1, keepdims=True)
    out = mm(mixed.astype(BF), v) + mm(p, dv) - row_sum * mm(p, v)
    probs[...] = p
    for i, value in enumerate((q, k, v)):
        primal[i] = value
    return out.astype(BF)


def near_kernel(gath, w_in, w_out, mods, tokens, term, primal, probs):
    blocks, _, rows, _ = gath.shape
    scale = 1.0 + mods[1:2, :]
    shift = mods[0:1, :]
    for i in range(blocks):
        normed, inverse = normalize(gath[i, 0].astype(F32))
        tokens[pl.ds(i * rows, rows), :] = (normed * scale + shift).astype(BF)
        field = norm_tangent(gath[i, 1].astype(F32), normed, inverse)
        tokens[pl.ds((blocks + i) * rows, rows), :] = (field * scale).astype(BF)
    term[...] = mm(head_forward(tokens, w_in, primal, probs), w_out[...])


def far_kernel(tokens, w_in, out, primal, probs):
    out[...] = head_forward(tokens, w_in, primal, probs)


def sum_kernel(term, out, w_out, parts):
    total = term[...] + mm(out[...], w_out[...])
    parts[...] = total.astype(BF).reshape(parts.shape)


def update_kernel(parts, probe, mods, gated, update):
    total = parts[0].astype(F32)
    for j in range(1, parts.shape[0]):
        total = total + parts[j].astype(F32)
    gate = mods[2:3, :]
    fresh = probe[0].astype(F32) + gate * total
    update[...] = fresh
    value = (gate * fresh).astype(BF)
    for j in range(gated.shape[0]):
        gated[j] = value


def adjoint_kernel(
    gated, near_in, near_out, near_primal, near_probs, far_in, far_out, far_primal, far_probs, parts
):
    c = HEAD_DIM ** (-0.5)
    blocks, rows, width = gated.shape
    whole = gated[...].reshape(blocks * rows, width)
    total = None
    for w_in, w_out, primal, probs in (
        (near_in, near_out, near_primal, near_probs),
        (far_in, far_out, far_primal, far_probs),
    ):
        co = mm(whole, w_out[...], NT).astype(BF)
        q, k, v = primal[0], primal[1], primal[2]
        p = probs[...]
        p_float = p.astype(F32)
        d_probs = mm(co, v, NT)
        row_dot = jnp.sum(p_float * d_probs, axis=-1, keepdims=True)
        scaled = (p_float * (d_probs - row_dot) * c).astype(BF)
        grads = (mm(scaled, k), mm(flip(scaled), q), mm(flip(p), co))
        grads = jnp.concatenate(grads, axis=1).astype(BF)
        term = mm(grads, w_in[...])
        total = term if total is None else total + term
    parts[...] = total.astype(BF).reshape(parts.shape)


def pulled_kernel(parts, update, noisy, mods, pulled, lost):
    total = parts[0].astype(F32)
    for j in range(1, parts.shape[0]):
        total = total + parts[j].astype(F32)
    normed, inverse = normalize(noisy[...].astype(F32))
    value = update[...] + norm_tangent((1.0 + mods[1:2, :]) * total, normed, inverse)
    rounded = value.astype(BF)
    lost[...] = value - rounded.astype(F32)
    pairs, each, _ = pulled.shape
    for i in range(pairs):
        pulled[i] = value[i * each : (i + 1) * each].astype(BF)


def gram_kernel(scale, mine, other, copies, rows):
    first = lax.axis_index("core") == 0
    for i in range(mine.shape[0]):
        rows[2 * i] = jnp.where(first, mine[i], other[i])
        rows[2 * i + 1] = jnp.where(first, other[i], mine[i])
    each = [rows[:, t, :] for t in range(rows.shape[1])]
    gram = sum(mm(row, row, NT) for row in each) * scale
    n = gram.shape[0]
    width = LANES // n
    high = n // width
    packed = jnp.concatenate([gram[i * high : (i + 1) * high] for i in range(width)], axis=1)
    for j in range(copies.shape[0]):
        copies[j] = packed


def tree_sum(terms):
    while len(terms) > 1:
        terms = [terms[i] + terms[i + 1] for i in range(0, len(terms), 2)]
    return terms[0]


def total_kernel(arrived, copies):
    total = tree_sum([arrived[j] for j in range(arrived.shape[0])])
    for j in range(copies.shape[0]):
        copies[j] = total


def picked(n, core):
    row = lax.broadcasted_iota(jnp.int32, (n // 2, n), 0)
    col = lax.broadcasted_iota(jnp.int32, (n // 2, n), 1)
    return jnp.where(col == 2 * row + core, 1.0, 0.0)


def solve_kernel(arrived, rows, lost, factor, solved, rest):
    packed = tree_sum([arrived[j] for j in range(arrived.shape[0])])
    n = factor.shape[0]
    width = LANES // n
    a = jnp.concatenate([packed[:, i * n : (i + 1) * n] for i in range(width)], axis=0)
    both = jnp.concatenate([a, eye(n)], axis=1)
    row = lax.broadcasted_iota(jnp.int32, both.shape, 0)
    col = lax.broadcasted_iota(jnp.int32, both.shape, 1)
    wide = (1, both.shape[1])
    for j in range(0, n, STEP):
        span = range(STEP)
        tops = [both[j + i : j + i + 1, :] for i in span]
        sides = [jnp.broadcast_to(both[:, j + i : j + i + 1], both.shape) for i in span]
        corner = [
            [jnp.broadcast_to(tops[i][:, j + k : j + k + 1], wide) for k in span] for i in span
        ]
        change = jnp.zeros_like(both)
        for i in span:
            inverse = 1.0 / corner[i][i]
            for k in range(i + 1, STEP):
                ratio = corner[i][k] * inverse
                tops[k] = tops[k] - ratio * tops[i]
                sides[k] = sides[k] - ratio * sides[i]
                for m in range(k, STEP):
                    corner[k][m] = corner[k][m] - ratio * corner[i][m]
            change = change + sides[i] * (tops[i] * inverse)
        below = both - jnp.where(row >= j + STEP, change, 0.0)
        for i in span:
            below = jnp.where(row == j + i, tops[i], below)
        both = below
    pivots = jnp.sum(jnp.where(row == col, both, 0.0), axis=1, keepdims=True)
    both = both / jnp.sqrt(pivots)
    factor[...] = jnp.where(col >= row, both, 0.0)[:, :n]
    core = lax.axis_index("core")
    own = lax.axis_index("z") * 2 + core
    square = jnp.where((row == own) & (col == own), both, 0.0)
    pivot = jnp.sum(jnp.sum(square, axis=0, keepdims=True), axis=1, keepdims=True)
    rest[...] = lost[...] * (1.0 / pivot)
    remains = both[:, n:]
    choice = picked(n, core).astype(BF)
    pieces = []
    for _ in range(3):
        piece = remains.astype(BF)
        pieces.append(mm(choice, piece))
        remains = remains - piece.astype(F32)
    pieces = jnp.concatenate(pieces, axis=0).astype(BF)
    for t in range(rows.shape[1]):
        product = mm(pieces, rows[:, t, :])
        high, middle, low = [product[i * n // 2 : (i + 1) * n // 2] for i in range(3)]
        solved[:, t, :] = (high + (middle + low)).astype(BF)


def basis_kernel(pairs, rest, triangle, basis, factor):
    factor[...] = triangle[...]
    count, each, _ = pairs.shape
    for i in range(count):
        at = slice(i * each, (i + 1) * each)
        basis[0, at, :] = pairs[i].astype(F32) + rest[at, :]


HBM = pl.BlockSpec(memory_space=pl.ANY)
LOCAL = pl.BlockSpec(memory_space=pltpu.VMEM)


def call(
    kernel, out_shape, *args, where=None, out_specs=None, scratch=(), flops=0, moved=0, limit=8
):
    return pl.pallas_call(
        kernel,
        out_shape=out_shape,
        in_specs=where or [LOCAL] * len(args),
        out_specs=out_specs or jax.tree.map(lambda _: LOCAL, out_shape),
        scratch_shapes=list(scratch),
        compiler_params=pltpu.CompilerParams(vmem_limit_bytes=limit * MIB),
        cost_estimate=pl.CostEstimate(flops=flops, bytes_accessed=moved, transcendentals=0),
    )(*args)


def exchange(blocks, axis):
    return lax.all_to_all(blocks, axis, split_axis=0, concat_axis=0, tiled=True)


def shards(noisy, probes, w_qkv, w_out, w_mod, timestep):
    rows, width = noisy.shape
    parts, frames, cores, chips = [lax.axis_size(n) for n in ("part", "frame", "core", "z")]
    seq_count = parts * frames
    probe_count = cores * chips
    frame_rows = parts * rows

    outgoing = call(
        copies_kernel,
        jax.ShapeDtypeStruct((parts, 2, rows, width), BF),
        noisy,
        probes,
        where=[HBM, HBM],
        out_specs=HBM,
        scratch=(
            pltpu.VMEM((2, rows, width), BF),
            pltpu.SemaphoreType.DMA((2 + parts,)),
        ),
        moved=2 * 10**6,
        limit=60,
    )
    outgoing, w_in, w_out = lax.optimization_barrier((outgoing, w_qkv.T, w_out))
    gath = exchange(outgoing, "part")
    half = seq_count - seq_count // 4
    partner = [(i, i ^ half) for i in range(seq_count)]
    far_in = lax.ppermute(w_in, SEQ, partner)
    far_out = lax.ppermute(w_out, SEQ, partner)
    mods = modulation(timestep, w_mod, width)

    part_sums = jax.ShapeDtypeStruct((parts, rows, width), BF)
    kept = (
        jax.ShapeDtypeStruct((3, frame_rows, HEAD_DIM), BF),
        jax.ShapeDtypeStruct((frame_rows, frame_rows), BF),
    )
    tokens, term, near_primal, near_probs = call(
        near_kernel,
        (
            jax.ShapeDtypeStruct((2 * frame_rows, width), BF),
            jax.ShapeDtypeStruct((frame_rows, width), F32),
        )
        + kept,
        gath,
        w_in,
        w_out,
        mods,
        flops=10**9,
        moved=6 * 10**6,
        limit=24,
    )
    out, far_primal, far_probs = call(
        far_kernel,
        (jax.ShapeDtypeStruct((frame_rows, HEAD_DIM), BF),) + kept,
        tokens,
        far_in,
        flops=10**9,
        moved=4 * 10**6,
        limit=24,
    )
    sums = call(sum_kernel, part_sums, term, out, far_out, flops=10**8, moved=10**6)
    sums = exchange(sums, "part")
    gated, update = call(
        update_kernel,
        (part_sums, jax.ShapeDtypeStruct((rows, width), F32)),
        sums,
        probes,
        mods,
        moved=10**6,
    )
    gated = exchange(gated, "part")
    sums = call(
        adjoint_kernel,
        part_sums,
        gated,
        w_in,
        w_out,
        near_primal,
        near_probs,
        far_in,
        far_out,
        far_primal,
        far_probs,
        flops=2 * 10**9,
        moved=5 * 10**6,
        limit=24,
    )
    sums = exchange(sums, "part")
    pairs = jax.ShapeDtypeStruct((chips, rows // chips, width), BF)
    own_rows = jax.ShapeDtypeStruct((rows, width), F32)
    pulled, lost = call(
        pulled_kernel, (pairs, own_rows), sums, update, noisy, mods, moved=10**6
    )
    mine = exchange(pulled, "z")
    other = lax.ppermute(mine, "core", [(i, i ^ 1) for i in range(cores)])
    high = probe_count * probe_count // LANES

    def blocks_of(count):
        return jax.ShapeDtypeStruct((count, high, LANES), F32)

    grams, every = call(
        functools.partial(gram_kernel, 1.0 / float(seq_count * rows * width)),
        (
            blocks_of(seq_count),
            jax.ShapeDtypeStruct((probe_count, rows // chips, width), BF),
        ),
        mine,
        other,
        moved=10**5,
    )
    grams = exchange(grams, SEQ)
    grams = call(total_kernel, blocks_of(chips), grams, moved=10**5)
    square = jax.ShapeDtypeStruct((probe_count, probe_count), F32)
    triangle, solved, rest = call(
        solve_kernel,
        (square, pairs, own_rows),
        exchange(grams, "z"),
        every,
        lost,
        moved=3 * 10**5,
    )
    basis, factor = call(
        basis_kernel,
        (jax.ShapeDtypeStruct((1, rows, width), F32), square),
        exchange(solved, "z"),
        rest,
        triangle,
        moved=3 * 10**5,
    )
    return basis, factor


def solution(mesh):
    split = Mesh(
        mesh.devices.reshape(
            mesh.shape["probe"] // 2, 2, FRAMES, mesh.shape["seq"] // FRAMES
        ),
        PROBE + SEQ,
    )
    placed = (P(SEQ, None), P(PROBE, SEQ, None), P(None, SEQ), P(SEQ, None), P(), P())
    return jax.shard_map(
        shards,
        mesh=split,
        in_specs=placed,
        out_specs=(P(PROBE, SEQ, None), P()),
        check_vma=False,
    )
```

```python
import functools
import math

import jax
import jax.numpy as jnp
from jax import lax
from jax.experimental import pallas as pl
from jax.experimental.pallas import tpu as pltpu
from jax.sharding import Mesh
from jax.sharding import PartitionSpec as P

HEAD_DIM = 72
LANES = 128
FRAMES = 2
SEQ = ("frame", "part")
PROBE = ("z", "core")
MIB = 1024 * 1024
STEP = 4
FEW = 16
NT = (((1,), (1,)), ((), ()))
NN = (((1,), (0,)), ((), ()))
BF = jnp.bfloat16
F32 = jnp.float32


def mm(a, b, dims=NN):
    return lax.dot_general(a, b, dims, preferred_element_type=F32)


def exact(a, b, dims=NN):
    return lax.dot_general(
        a, b, dims, precision=lax.Precision.HIGHEST, preferred_element_type=F32
    )


def eye(n):
    row = lax.broadcasted_iota(jnp.int32, (n, n), 0)
    col = lax.broadcasted_iota(jnp.int32, (n, n), 1)
    return jnp.where(row == col, 1.0, 0.0)


def flip(a):
    return mm(eye(a.shape[1]).astype(BF), a, NT).astype(BF)


def modulation(timestep, w_mod, feat_width):
    half_dim = w_mod.shape[0] // 2
    freq_index = jnp.arange(half_dim, dtype=jnp.float32)
    frequency = jnp.exp(-math.log(10000.0) * freq_index / half_dim)
    angles = timestep[0].astype(jnp.float32) * frequency
    embedding = jnp.concatenate([jnp.cos(angles), jnp.sin(angles)])
    modulated = jnp.dot(
        jax.nn.silu(embedding)[None, :], w_mod.astype(jnp.float32), precision=lax.Precision.HIGHEST
    )
    return modulated.reshape(3, feat_width)


def normalize(values_f):
    centered = values_f - jnp.mean(values_f, axis=-1, keepdims=True)
    inverse = 1.0 / jnp.sqrt(jnp.mean(centered * centered, axis=-1, keepdims=True) + 1e-06)
    return centered * inverse, inverse


def norm_tangent(field, normed, inverse):
    mean_part = jnp.mean(field, axis=-1, keepdims=True)
    along = jnp.mean(field * normed, axis=-1, keepdims=True)
    return (field - mean_part - normed * along) * inverse


def fetch(pairs, sems):
    copies = [pltpu.make_async_copy(a, b, sems.at[i]) for i, (a, b) in enumerate(pairs)]
    for copy in copies:
        copy.start()
    return copies


def copies_kernel(noisy, probe, out, staged, sems):
    count = out.shape[0]
    for copy in fetch([(noisy, staged.at[0]), (probe.at[0], staged.at[1])], sems):
        copy.wait()
    for copy in fetch([(staged, out.at[j]) for j in range(count)], sems.at[pl.ds(2, count)]):
        copy.wait()


def thirds(value):
    return [value[:, i * HEAD_DIM : (i + 1) * HEAD_DIM].astype(BF) for i in range(3)]


def head_forward(tokens, w_in, primal, probs):
    c = HEAD_DIM ** (-0.5)
    count = tokens.shape[0] // 2
    projected = mm(tokens[...], w_in[...], NT)
    q, k, v = thirds(projected[:count])
    dq, dk, dv = thirds(projected[count:])
    scores = mm(q, k, NT) * c
    expon = jnp.exp(scores - jnp.max(scores, axis=-1, keepdims=True))
    p = (expon * (1.0 / jnp.sum(expon, axis=-1, keepdims=True))).astype(BF)
    d_scores = (mm(dq, k, NT) + mm(q, dk, NT)) * c
    mixed = p.astype(F32) * d_scores
    row_sum = jnp.sum(mixed, axis=-1, keepdims=True)
    out = mm(mixed.astype(BF), v) + mm(p, dv) - row_sum * mm(p, v)
    probs[...] = p
    for i, value in enumerate((q, k, v)):
        primal[i] = value
    return out.astype(BF)


def near_kernel(gath, w_in, w_out, mods, tokens, term, primal, probs):
    blocks, _, rows, _ = gath.shape
    scale = 1.0 + mods[1:2, :]
    shift = mods[0:1, :]
    for i in range(blocks):
        for at in range(0, rows, FEW):
            few = pl.ds(at, FEW)
            normed, inverse = normalize(gath[i, 0, few, :].astype(F32))
            tokens[pl.ds(i * rows + at, FEW), :] = (normed * scale + shift).astype(BF)
            field = norm_tangent(gath[i, 1, few, :].astype(F32), normed, inverse)
            tokens[pl.ds((blocks + i) * rows + at, FEW), :] = (field * scale).astype(BF)
    term[...] = mm(head_forward(tokens, w_in, primal, probs), w_out[...])


def far_kernel(tokens, w_in, out, primal, probs):
    out[...] = head_forward(tokens, w_in, primal, probs)


def sum_kernel(term, out, w_out, parts):
    total = term[...] + mm(out[...], w_out[...])
    parts[...] = total.astype(BF).reshape(parts.shape)


def update_kernel(parts, probe, mods, gated, update):
    total = parts[0].astype(F32)
    for j in range(1, parts.shape[0]):
        total = total + parts[j].astype(F32)
    gate = mods[2:3, :]
    fresh = probe[0].astype(F32) + gate * total
    update[...] = fresh
    value = (gate * fresh).astype(BF)
    for j in range(gated.shape[0]):
        gated[j] = value


def adjoint_kernel(
    gated,
    near_in,
    near_out,
    near_primal,
    near_probs,
    far_in,
    far_out,
    far_primal,
    far_probs,
    parts,
    w_in,
):
    c = HEAD_DIM ** (-0.5)
    blocks, rows, width = gated.shape
    whole = gated[...].reshape(blocks * rows, width)
    third = 3 * HEAD_DIM
    w_in[pl.ds(0, third), :] = near_in[...].astype(F32)
    w_in[pl.ds(third, third), :] = far_in[...].astype(F32)
    grads = []
    for w_out, primal, probs in (
        (near_out, near_primal, near_probs),
        (far_out, far_primal, far_probs),
    ):
        co = mm(whole, w_out[...], NT).astype(BF)
        q, k, v = primal[0], primal[1], primal[2]
        p = probs[...]
        p_float = p.astype(F32)
        d_probs = mm(co, v, NT)
        row_dot = jnp.sum(p_float * d_probs, axis=-1, keepdims=True)
        scaled = (p_float * (d_probs - row_dot) * c).astype(BF)
        grads += [mm(scaled, k), mm(flip(scaled), q), mm(flip(p), co)]
    grads = jnp.concatenate(grads, axis=1).astype(BF)
    parts[...] = mm(grads, w_in[...].astype(BF)).astype(BF).reshape(parts.shape)


def pulled_kernel(parts, update, noisy, mods, pulled, lost):
    total = parts[0].astype(F32)
    for j in range(1, parts.shape[0]):
        total = total + parts[j].astype(F32)
    normed, inverse = normalize(noisy[...].astype(F32))
    value = update[...] + norm_tangent((1.0 + mods[1:2, :]) * total, normed, inverse)
    rounded = value.astype(BF)
    lost[...] = value - rounded.astype(F32)
    pairs, each, _ = pulled.shape
    for i in range(pairs):
        pulled[i] = value[i * each : (i + 1) * each].astype(BF)


def gram_kernel(scale, mine, other, copies, rows):
    first = lax.axis_index("core") == 0
    for i in range(mine.shape[0]):
        rows[2 * i] = jnp.where(first, mine[i], other[i])
        rows[2 * i + 1] = jnp.where(first, other[i], mine[i])
    each = [rows[:, t, :] for t in range(rows.shape[1])]
    gram = sum(mm(row, row, NT) for row in each) * scale
    n = gram.shape[0]
    width = LANES // n
    high = n // width
    packed = jnp.concatenate([gram[i * high : (i + 1) * high] for i in range(width)], axis=1)
    for j in range(copies.shape[0]):
        copies[j] = packed


def tree_sum(terms):
    while len(terms) > 1:
        terms = [terms[i] + terms[i + 1] for i in range(0, len(terms), 2)]
    return terms[0]


def total_kernel(arrived, copies):
    total = tree_sum([arrived[j] for j in range(arrived.shape[0])])
    for j in range(copies.shape[0]):
        copies[j] = total


def picked(n, core):
    row = lax.broadcasted_iota(jnp.int32, (n // 2, n), 0)
    col = lax.broadcasted_iota(jnp.int32, (n // 2, n), 1)
    return jnp.where(col == 2 * row + core, 1.0, 0.0)


def solve_kernel(arrived, rows, lost, factor, solved, rest):
    packed = tree_sum([arrived[j] for j in range(arrived.shape[0])])
    n = factor.shape[0]
    width = LANES // n
    a = jnp.concatenate([packed[:, i * n : (i + 1) * n] for i in range(width)], axis=0)
    both = jnp.concatenate([a, eye(n)], axis=1)
    row = lax.broadcasted_iota(jnp.int32, both.shape, 0)
    col = lax.broadcasted_iota(jnp.int32, both.shape, 1)
    wide = (1, both.shape[1])
    for j in range(0, n, STEP):
        span = range(STEP)
        tops = [both[j + i : j + i + 1, :] for i in span]
        sides = [jnp.broadcast_to(both[:, j + i : j + i + 1], both.shape) for i in span]
        corner = [
            [jnp.broadcast_to(tops[i][:, j + k : j + k + 1], wide) for k in span] for i in span
        ]
        change = jnp.zeros_like(both)
        for i in span:
            inverse = 1.0 / corner[i][i]
            for k in range(i + 1, STEP):
                ratio = corner[i][k] * inverse
                tops[k] = tops[k] - ratio * tops[i]
                sides[k] = sides[k] - ratio * sides[i]
                for m in range(k, STEP):
                    corner[k][m] = corner[k][m] - ratio * corner[i][m]
            change = change + sides[i] * (tops[i] * inverse)
        below = both - jnp.where(row >= j + STEP, change, 0.0)
        for i in span:
            below = jnp.where(row == j + i, tops[i], below)
        both = below
    pivots = jnp.sum(jnp.where(row == col, both, 0.0), axis=1, keepdims=True)
    both = both / jnp.sqrt(pivots)
    factor[...] = jnp.where(col >= row, both, 0.0)[:, :n]
    core = lax.axis_index("core")
    own = lax.axis_index("z") * 2 + core
    square = jnp.where((row == own) & (col == own), both, 0.0)
    pivot = jnp.sum(jnp.sum(square, axis=0, keepdims=True), axis=1, keepdims=True)
    rest[...] = lost[...] * (1.0 / pivot)
    remains = both[:, n:]
    choice = picked(n, core).astype(BF)
    pieces = []
    for _ in range(3):
        piece = remains.astype(BF)
        pieces.append(mm(choice, piece))
        remains = remains - piece.astype(F32)
    pieces = jnp.concatenate(pieces, axis=0).astype(BF)
    for t in range(rows.shape[1]):
        product = mm(pieces, rows[:, t, :])
        high, middle, low = [product[i * n // 2 : (i + 1) * n // 2] for i in range(3)]
        solved[:, t, :] = (high + (middle + low)).astype(BF)


def basis_kernel(pairs, rest, triangle, basis, factor):
    factor[...] = triangle[...]
    count, each, _ = pairs.shape
    for i in range(count):
        at = slice(i * each, (i + 1) * each)
        basis[0, at, :] = pairs[i].astype(F32) + rest[at, :]


HBM = pl.BlockSpec(memory_space=pl.ANY)
LOCAL = pl.BlockSpec(memory_space=pltpu.VMEM)


def call(
    kernel, out_shape, *args, where=None, out_specs=None, scratch=(), flops=0, moved=0, limit=8
):
    return pl.pallas_call(
        kernel,
        out_shape=out_shape,
        in_specs=where or [LOCAL] * len(args),
        out_specs=out_specs or jax.tree.map(lambda _: LOCAL, out_shape),
        scratch_shapes=list(scratch),
        compiler_params=pltpu.CompilerParams(vmem_limit_bytes=limit * MIB),
        cost_estimate=pl.CostEstimate(flops=flops, bytes_accessed=moved, transcendentals=0),
    )(*args)


def exchange(blocks, axis):
    return lax.all_to_all(blocks, axis, split_axis=0, concat_axis=0, tiled=True)


def shards(noisy, probes, w_qkv, w_out, w_mod, timestep):
    rows, width = noisy.shape
    parts, frames, cores, chips = [lax.axis_size(n) for n in ("part", "frame", "core", "z")]
    seq_count = parts * frames
    probe_count = cores * chips
    frame_rows = parts * rows

    outgoing = call(
        copies_kernel,
        jax.ShapeDtypeStruct((parts, 2, rows, width), BF),
        noisy,
        probes,
        where=[HBM, HBM],
        out_specs=HBM,
        scratch=(
            pltpu.VMEM((2, rows, width), BF),
            pltpu.SemaphoreType.DMA((2 + parts,)),
        ),
        moved=2 * 10**6,
        limit=60,
    )
    outgoing, w_in, w_out = lax.optimization_barrier((outgoing, w_qkv.T, w_out))
    gath = exchange(outgoing, "part")
    half = seq_count - seq_count // 4
    partner = [(i, i ^ half) for i in range(seq_count)]
    far_in = lax.ppermute(w_in, SEQ, partner)
    far_out = lax.ppermute(w_out, SEQ, partner)
    mods = modulation(timestep, w_mod, width)

    part_sums = jax.ShapeDtypeStruct((parts, rows, width), BF)
    kept = (
        jax.ShapeDtypeStruct((3, frame_rows, HEAD_DIM), BF),
        jax.ShapeDtypeStruct((frame_rows, frame_rows), BF),
    )
    tokens, term, near_primal, near_probs = call(
        near_kernel,
        (
            jax.ShapeDtypeStruct((2 * frame_rows, width), BF),
            jax.ShapeDtypeStruct((frame_rows, width), F32),
        )
        + kept,
        gath,
        w_in,
        w_out,
        mods,
        flops=10**9,
        moved=6 * 10**6,
        limit=24,
    )
    out, far_primal, far_probs = call(
        far_kernel,
        (jax.ShapeDtypeStruct((frame_rows, HEAD_DIM), BF),) + kept,
        tokens,
        far_in,
        flops=10**9,
        moved=4 * 10**6,
        limit=24,
    )
    sums = call(sum_kernel, part_sums, term, out, far_out, flops=10**8, moved=10**6)
    sums = exchange(sums, "part")
    gated, update = call(
        update_kernel,
        (part_sums, jax.ShapeDtypeStruct((rows, width), F32)),
        sums,
        probes,
        mods,
        moved=10**6,
    )
    gated = exchange(gated, "part")
    sums = call(
        adjoint_kernel,
        part_sums,
        gated,
        w_in,
        w_out,
        near_primal,
        near_probs,
        far_in,
        far_out,
        far_primal,
        far_probs,
        scratch=(pltpu.VMEM((6 * HEAD_DIM, width), F32),),
        flops=2 * 10**9,
        moved=5 * 10**6,
        limit=24,
    )
    sums = exchange(sums, "part")
    pairs = jax.ShapeDtypeStruct((chips, rows // chips, width), BF)
    own_rows = jax.ShapeDtypeStruct((rows, width), F32)
    pulled, lost = call(
        pulled_kernel, (pairs, own_rows), sums, update, noisy, mods, moved=10**6
    )
    mine = exchange(pulled, "z")
    other = lax.ppermute(mine, "core", [(i, i ^ 1) for i in range(cores)])
    high = probe_count * probe_count // LANES

    def blocks_of(count):
        return jax.ShapeDtypeStruct((count, high, LANES), F32)

    grams, every = call(
        functools.partial(gram_kernel, 1.0 / float(seq_count * rows * width)),
        (
            blocks_of(seq_count),
            jax.ShapeDtypeStruct((probe_count, rows // chips, width), BF),
        ),
        mine,
        other,
        moved=10**5,
    )
    grams = exchange(grams, SEQ)
    grams = call(total_kernel, blocks_of(chips), grams, moved=10**5)
    square = jax.ShapeDtypeStruct((probe_count, probe_count), F32)
    triangle, solved, rest = call(
        solve_kernel,
        (square, pairs, own_rows),
        exchange(grams, "z"),
        every,
        lost,
        moved=3 * 10**5,
    )
    basis, factor = call(
        basis_kernel,
        (jax.ShapeDtypeStruct((1, rows, width), F32), square),
        exchange(solved, "z"),
        rest,
        triangle,
        moved=3 * 10**5,
    )
    return basis, factor


def solution(mesh):
    split = Mesh(
        mesh.devices.reshape(
            mesh.shape["probe"] // 2, 2, FRAMES, mesh.shape["seq"] // FRAMES
        ),
        PROBE + SEQ,
    )
    placed = (P(SEQ, None), P(PROBE, SEQ, None), P(None, SEQ), P(SEQ, None), P(), P())
    return jax.shard_map(
        shards,
        mesh=split,
        in_specs=placed,
        out_specs=(P(PROBE, SEQ, None), P()),
        check_vma=False,
    )
```

```python
import functools
import math

import jax
import jax.numpy as jnp
from jax import lax
from jax.experimental import pallas as pl
from jax.experimental.pallas import tpu as pltpu
from jax.sharding import Mesh
from jax.sharding import PartitionSpec as P

HEAD_DIM = 72
LANES = 128
FRAMES = 2
SEQ = ("frame", "part")
PROBE = ("z", "core")
MIB = 1024 * 1024
STEP = 4
FEW = 16
NT = (((1,), (1,)), ((), ()))
NN = (((1,), (0,)), ((), ()))
BF = jnp.bfloat16
F32 = jnp.float32


def mm(a, b, dims=NN):
    return lax.dot_general(a, b, dims, preferred_element_type=F32)


def exact(a, b, dims=NN):
    return lax.dot_general(
        a, b, dims, precision=lax.Precision.HIGHEST, preferred_element_type=F32
    )


def eye(n):
    row = lax.broadcasted_iota(jnp.int32, (n, n), 0)
    col = lax.broadcasted_iota(jnp.int32, (n, n), 1)
    return jnp.where(row == col, 1.0, 0.0)


def flip(a):
    return mm(eye(a.shape[1]).astype(BF), a, NT).astype(BF)


def modulation(timestep, w_mod, feat_width):
    half_dim = w_mod.shape[0] // 2
    freq_index = jnp.arange(half_dim, dtype=jnp.float32)
    frequency = jnp.exp(-math.log(10000.0) * freq_index / half_dim)
    angles = timestep[0].astype(jnp.float32) * frequency
    embedding = jnp.concatenate([jnp.cos(angles), jnp.sin(angles)])
    modulated = jnp.sum(jax.nn.silu(embedding)[:, None] * w_mod.astype(jnp.float32), axis=0)
    return modulated.reshape(3, feat_width)


def normalize(values_f):
    centered = values_f - jnp.mean(values_f, axis=-1, keepdims=True)
    inverse = 1.0 / jnp.sqrt(jnp.mean(centered * centered, axis=-1, keepdims=True) + 1e-06)
    return centered * inverse, inverse


def norm_tangent(field, normed, inverse):
    mean_part = jnp.mean(field, axis=-1, keepdims=True)
    along = jnp.mean(field * normed, axis=-1, keepdims=True)
    return (field - mean_part - normed * along) * inverse


def fetch(pairs, sems):
    copies = [pltpu.make_async_copy(a, b, sems.at[i]) for i, (a, b) in enumerate(pairs)]
    for copy in copies:
        copy.start()
    return copies


def copies_kernel(noisy, probe, out, staged, sems):
    count = out.shape[0]
    for copy in fetch([(noisy, staged.at[0]), (probe.at[0], staged.at[1])], sems):
        copy.wait()
    for copy in fetch([(staged, out.at[j]) for j in range(count)], sems.at[pl.ds(2, count)]):
        copy.wait()


def thirds(value):
    return [value[:, i * HEAD_DIM : (i + 1) * HEAD_DIM].astype(BF) for i in range(3)]


def head_forward(tokens, w_in, primal, probs):
    c = HEAD_DIM ** (-0.5)
    count = tokens.shape[0] // 2
    projected = mm(tokens[...], w_in[...], NT)
    q, k, v = thirds(projected[:count])
    dq, dk, dv = thirds(projected[count:])
    scores = mm(q, k, NT) * c
    expon = jnp.exp(scores - jnp.max(scores, axis=-1, keepdims=True))
    p = (expon * (1.0 / jnp.sum(expon, axis=-1, keepdims=True))).astype(BF)
    d_scores = (mm(dq, k, NT) + mm(q, dk, NT)) * c
    mixed = p.astype(F32) * d_scores
    row_sum = jnp.sum(mixed, axis=-1, keepdims=True)
    out = mm(mixed.astype(BF), v) + mm(p, dv) - row_sum * mm(p, v)
    probs[...] = p
    for i, value in enumerate((q, k, v)):
        primal[i] = value
    return out.astype(BF)


def near_kernel(gath, w_in, w_out, mods, tokens, term, primal, probs):
    blocks, _, rows, _ = gath.shape
    scale = 1.0 + mods[1:2, :]
    shift = mods[0:1, :]
    for i in range(blocks):
        for at in range(0, rows, FEW):
            few = pl.ds(at, FEW)
            normed, inverse = normalize(gath[i, 0, few, :].astype(F32))
            tokens[pl.ds(i * rows + at, FEW), :] = (normed * scale + shift).astype(BF)
            field = norm_tangent(gath[i, 1, few, :].astype(F32), normed, inverse)
            tokens[pl.ds((blocks + i) * rows + at, FEW), :] = (field * scale).astype(BF)
    term[...] = mm(head_forward(tokens, w_in, primal, probs), w_out[...])


def far_kernel(tokens, w_in, out, primal, probs):
    out[...] = head_forward(tokens, w_in, primal, probs)


def sum_kernel(term, out, w_out, parts):
    total = term[...] + mm(out[...], w_out[...])
    parts[...] = total.astype(BF).reshape(parts.shape)


def update_kernel(parts, probe, mods, gated, update):
    total = parts[0].astype(F32)
    for j in range(1, parts.shape[0]):
        total = total + parts[j].astype(F32)
    gate = mods[2:3, :]
    fresh = probe[0].astype(F32) + gate * total
    update[...] = fresh
    value = (gate * fresh).astype(BF)
    for j in range(gated.shape[0]):
        gated[j] = value


def adjoint_kernel(
    gated,
    near_in,
    near_out,
    near_primal,
    near_probs,
    far_in,
    far_out,
    far_primal,
    far_probs,
    parts,
    w_in,
):
    c = HEAD_DIM ** (-0.5)
    blocks, rows, width = gated.shape
    whole = gated[...].reshape(blocks * rows, width)
    third = 3 * HEAD_DIM
    w_in[pl.ds(0, third), :] = near_in[...].astype(F32)
    w_in[pl.ds(third, third), :] = far_in[...].astype(F32)
    grads = []
    for w_out, primal, probs in (
        (near_out, near_primal, near_probs),
        (far_out, far_primal, far_probs),
    ):
        co = mm(whole, w_out[...], NT).astype(BF)
        q, k, v = primal[0], primal[1], primal[2]
        p = probs[...]
        p_float = p.astype(F32)
        d_probs = mm(co, v, NT)
        row_dot = jnp.sum(p_float * d_probs, axis=-1, keepdims=True)
        scaled = (p_float * (d_probs - row_dot) * c).astype(BF)
        grads += [mm(scaled, k), mm(flip(scaled), q), mm(flip(p), co)]
    grads = jnp.concatenate(grads, axis=1).astype(BF)
    parts[...] = mm(grads, w_in[...].astype(BF)).astype(BF).reshape(parts.shape)


def pulled_kernel(parts, update, noisy, mods, pulled, lost):
    total = parts[0].astype(F32)
    for j in range(1, parts.shape[0]):
        total = total + parts[j].astype(F32)
    normed, inverse = normalize(noisy[...].astype(F32))
    value = update[...] + norm_tangent((1.0 + mods[1:2, :]) * total, normed, inverse)
    rounded = value.astype(BF)
    lost[...] = value - rounded.astype(F32)
    pairs, each, _ = pulled.shape
    for i in range(pairs):
        pulled[i] = value[i * each : (i + 1) * each].astype(BF)


def gram_kernel(scale, mine, other, copies, rows):
    first = lax.axis_index("core") == 0
    for i in range(mine.shape[0]):
        rows[2 * i] = jnp.where(first, mine[i], other[i])
        rows[2 * i + 1] = jnp.where(first, other[i], mine[i])
    each = [rows[:, t, :] for t in range(rows.shape[1])]
    gram = sum(mm(row, row, NT) for row in each) * scale
    n = gram.shape[0]
    width = LANES // n
    high = n // width
    packed = jnp.concatenate([gram[i * high : (i + 1) * high] for i in range(width)], axis=1)
    for j in range(copies.shape[0]):
        copies[j] = packed


def tree_sum(terms):
    while len(terms) > 1:
        terms = [terms[i] + terms[i + 1] for i in range(0, len(terms), 2)]
    return terms[0]


def total_kernel(arrived, copies):
    total = tree_sum([arrived[j] for j in range(arrived.shape[0])])
    for j in range(copies.shape[0]):
        copies[j] = total


def picked(n, core):
    row = lax.broadcasted_iota(jnp.int32, (n // 2, n), 0)
    col = lax.broadcasted_iota(jnp.int32, (n // 2, n), 1)
    return jnp.where(col == 2 * row + core, 1.0, 0.0)


def solve_kernel(arrived, rows, lost, factor, solved, rest):
    packed = tree_sum([arrived[j] for j in range(arrived.shape[0])])
    n = factor.shape[0]
    width = LANES // n
    a = jnp.concatenate([packed[:, i * n : (i + 1) * n] for i in range(width)], axis=0)
    both = jnp.concatenate([a, eye(n)], axis=1)
    row = lax.broadcasted_iota(jnp.int32, both.shape, 0)
    col = lax.broadcasted_iota(jnp.int32, both.shape, 1)
    wide = (1, both.shape[1])
    for j in range(0, n, STEP):
        span = range(STEP)
        tops = [both[j + i : j + i + 1, :] for i in span]
        sides = [jnp.broadcast_to(both[:, j + i : j + i + 1], both.shape) for i in span]
        corner = [
            [jnp.broadcast_to(tops[i][:, j + k : j + k + 1], wide) for k in span] for i in span
        ]
        change = jnp.zeros_like(both)
        for i in span:
            inverse = 1.0 / corner[i][i]
            for k in range(i + 1, STEP):
                ratio = corner[i][k] * inverse
                tops[k] = tops[k] - ratio * tops[i]
                sides[k] = sides[k] - ratio * sides[i]
                for m in range(k, STEP):
                    corner[k][m] = corner[k][m] - ratio * corner[i][m]
            change = change + sides[i] * (tops[i] * inverse)
        below = both - jnp.where(row >= j + STEP, change, 0.0)
        for i in span:
            below = jnp.where(row == j + i, tops[i], below)
        both = below
    pivots = jnp.sum(jnp.where(row == col, both, 0.0), axis=1, keepdims=True)
    both = both / jnp.sqrt(pivots)
    factor[...] = jnp.where(col >= row, both, 0.0)[:, :n]
    core = lax.axis_index("core")
    own = lax.axis_index("z") * 2 + core
    square = jnp.where((row == own) & (col == own), both, 0.0)
    pivot = jnp.sum(jnp.sum(square, axis=0, keepdims=True), axis=1, keepdims=True)
    rest[...] = lost[...] * (1.0 / pivot)
    remains = both[:, n:]
    choice = picked(n, core).astype(BF)
    pieces = []
    for _ in range(3):
        piece = remains.astype(BF)
        pieces.append(mm(choice, piece))
        remains = remains - piece.astype(F32)
    pieces = jnp.concatenate(pieces, axis=0).astype(BF)
    for t in range(rows.shape[1]):
        product = mm(pieces, rows[:, t, :])
        high, middle, low = [product[i * n // 2 : (i + 1) * n // 2] for i in range(3)]
        solved[:, t, :] = (high + (middle + low)).astype(BF)


def basis_kernel(pairs, rest, triangle, basis, factor):
    factor[...] = triangle[...]
    count, each, _ = pairs.shape
    for i in range(count):
        at = slice(i * each, (i + 1) * each)
        basis[0, at, :] = pairs[i].astype(F32) + rest[at, :]


HBM = pl.BlockSpec(memory_space=pl.ANY)
LOCAL = pl.BlockSpec(memory_space=pltpu.VMEM)


def call(
    kernel, out_shape, *args, where=None, out_specs=None, scratch=(), flops=0, moved=0, limit=8
):
    return pl.pallas_call(
        kernel,
        out_shape=out_shape,
        in_specs=where or [LOCAL] * len(args),
        out_specs=out_specs or jax.tree.map(lambda _: LOCAL, out_shape),
        scratch_shapes=list(scratch),
        compiler_params=pltpu.CompilerParams(vmem_limit_bytes=limit * MIB),
        cost_estimate=pl.CostEstimate(flops=flops, bytes_accessed=moved, transcendentals=0),
    )(*args)


def exchange(blocks, axis):
    return lax.all_to_all(blocks, axis, split_axis=0, concat_axis=0, tiled=True)


def shards(noisy, probes, w_qkv, w_out, w_mod, timestep):
    rows, width = noisy.shape
    parts, frames, cores, chips = [lax.axis_size(n) for n in ("part", "frame", "core", "z")]
    seq_count = parts * frames
    probe_count = cores * chips
    frame_rows = parts * rows

    outgoing = call(
        copies_kernel,
        jax.ShapeDtypeStruct((parts, 2, rows, width), BF),
        noisy,
        probes,
        where=[HBM, HBM],
        out_specs=HBM,
        scratch=(
            pltpu.VMEM((2, rows, width), BF),
            pltpu.SemaphoreType.DMA((2 + parts,)),
        ),
        moved=2 * 10**6,
        limit=60,
    )
    outgoing, w_in, w_out = lax.optimization_barrier((outgoing, w_qkv.T, w_out))
    gath = exchange(outgoing, "part")
    half = seq_count - seq_count // 4
    partner = [(i, i ^ half) for i in range(seq_count)]
    far_in = lax.ppermute(w_in, SEQ, partner)
    far_out = lax.ppermute(w_out, SEQ, partner)
    mods = modulation(timestep, w_mod, width)

    part_sums = jax.ShapeDtypeStruct((parts, rows, width), BF)
    kept = (
        jax.ShapeDtypeStruct((3, frame_rows, HEAD_DIM), BF),
        jax.ShapeDtypeStruct((frame_rows, frame_rows), BF),
    )
    tokens, term, near_primal, near_probs = call(
        near_kernel,
        (
            jax.ShapeDtypeStruct((2 * frame_rows, width), BF),
            jax.ShapeDtypeStruct((frame_rows, width), F32),
        )
        + kept,
        gath,
        w_in,
        w_out,
        mods,
        flops=10**9,
        moved=6 * 10**6,
        limit=24,
    )
    out, far_primal, far_probs = call(
        far_kernel,
        (jax.ShapeDtypeStruct((frame_rows, HEAD_DIM), BF),) + kept,
        tokens,
        far_in,
        flops=10**9,
        moved=4 * 10**6,
        limit=24,
    )
    sums = call(sum_kernel, part_sums, term, out, far_out, flops=10**8, moved=10**6)
    sums = exchange(sums, "part")
    gated, update = call(
        update_kernel,
        (part_sums, jax.ShapeDtypeStruct((rows, width), F32)),
        sums,
        probes,
        mods,
        moved=10**6,
    )
    gated = exchange(gated, "part")
    sums = call(
        adjoint_kernel,
        part_sums,
        gated,
        w_in,
        w_out,
        near_primal,
        near_probs,
        far_in,
        far_out,
        far_primal,
        far_probs,
        scratch=(pltpu.VMEM((6 * HEAD_DIM, width), F32),),
        flops=2 * 10**9,
        moved=5 * 10**6,
        limit=24,
    )
    sums = exchange(sums, "part")
    pairs = jax.ShapeDtypeStruct((chips, rows // chips, width), BF)
    own_rows = jax.ShapeDtypeStruct((rows, width), F32)
    pulled, lost = call(
        pulled_kernel, (pairs, own_rows), sums, update, noisy, mods, moved=10**6
    )
    mine = exchange(pulled, "z")
    other = lax.ppermute(mine, "core", [(i, i ^ 1) for i in range(cores)])
    high = probe_count * probe_count // LANES

    def blocks_of(count):
        return jax.ShapeDtypeStruct((count, high, LANES), F32)

    grams, every = call(
        functools.partial(gram_kernel, 1.0 / float(seq_count * rows * width)),
        (
            blocks_of(seq_count),
            jax.ShapeDtypeStruct((probe_count, rows // chips, width), BF),
        ),
        mine,
        other,
        moved=10**5,
    )
    grams = exchange(grams, SEQ)
    grams = call(total_kernel, blocks_of(chips), grams, moved=10**5)
    square = jax.ShapeDtypeStruct((probe_count, probe_count), F32)
    triangle, solved, rest = call(
        solve_kernel,
        (square, pairs, own_rows),
        exchange(grams, "z"),
        every,
        lost,
        moved=3 * 10**5,
    )
    basis, factor = call(
        basis_kernel,
        (jax.ShapeDtypeStruct((1, rows, width), F32), square),
        exchange(solved, "z"),
        rest,
        triangle,
        moved=3 * 10**5,
    )
    return basis, factor


def solution(mesh):
    split = Mesh(
        mesh.devices.reshape(
            mesh.shape["probe"] // 2, 2, FRAMES, mesh.shape["seq"] // FRAMES
        ),
        PROBE + SEQ,
    )
    placed = (P(SEQ, None), P(PROBE, SEQ, None), P(None, SEQ), P(SEQ, None), P(), P())
    return jax.shard_map(
        shards,
        mesh=split,
        in_specs=placed,
        out_specs=(P(PROBE, SEQ, None), P()),
        check_vma=False,
    )
```

```python
import functools
import math

import jax
import jax.numpy as jnp
from jax import lax
from jax.experimental import pallas as pl
from jax.experimental.pallas import tpu as pltpu
from jax.sharding import Mesh
from jax.sharding import PartitionSpec as P

HEAD_DIM = 72
LANES = 128
FRAMES = 2
SEQ = ("frame", "part")
PROBE = ("z", "core")
MIB = 1024 * 1024
STEP = 4
FEW = 16
NT = (((1,), (1,)), ((), ()))
NN = (((1,), (0,)), ((), ()))
TN = (((0,), (0,)), ((), ()))
BF = jnp.bfloat16
F32 = jnp.float32


def mm(a, b, dims=NN):
    return lax.dot_general(a, b, dims, preferred_element_type=F32)


def exact(a, b, dims=NN):
    return lax.dot_general(
        a, b, dims, precision=lax.Precision.HIGHEST, preferred_element_type=F32
    )


def eye(n):
    row = lax.broadcasted_iota(jnp.int32, (n, n), 0)
    col = lax.broadcasted_iota(jnp.int32, (n, n), 1)
    return jnp.where(row == col, 1.0, 0.0)


def modulation(timestep, w_mod, feat_width):
    half_dim = w_mod.shape[0] // 2
    freq_index = jnp.arange(half_dim, dtype=jnp.float32)
    frequency = jnp.exp(-math.log(10000.0) * freq_index / half_dim)
    angles = timestep[0].astype(jnp.float32) * frequency
    embedding = jnp.concatenate([jnp.cos(angles), jnp.sin(angles)])
    modulated = jnp.sum(jax.nn.silu(embedding)[:, None] * w_mod.astype(jnp.float32), axis=0)
    return modulated.reshape(3, feat_width)


def normalize(values_f):
    centered = values_f - jnp.mean(values_f, axis=-1, keepdims=True)
    inverse = 1.0 / jnp.sqrt(jnp.mean(centered * centered, axis=-1, keepdims=True) + 1e-06)
    return centered * inverse, inverse


def norm_tangent(field, normed, inverse):
    mean_part = jnp.mean(field, axis=-1, keepdims=True)
    along = jnp.mean(field * normed, axis=-1, keepdims=True)
    return (field - mean_part - normed * along) * inverse


def fetch(pairs, sems):
    copies = [pltpu.make_async_copy(a, b, sems.at[i]) for i, (a, b) in enumerate(pairs)]
    for copy in copies:
        copy.start()
    return copies


def copies_kernel(noisy, probe, out, staged, sems):
    count = out.shape[0]
    for copy in fetch([(noisy, staged.at[0]), (probe.at[0], staged.at[1])], sems):
        copy.wait()
    for copy in fetch([(staged, out.at[j]) for j in range(count)], sems.at[pl.ds(2, count)]):
        copy.wait()


def thirds(value):
    return [value[:, i * HEAD_DIM : (i + 1) * HEAD_DIM].astype(BF) for i in range(3)]


def head_forward(projected, primal, probs):
    c = HEAD_DIM ** (-0.5)
    count = projected.shape[0] // 2
    q, k, v = thirds(projected[:count])
    dq, dk, dv = thirds(projected[count:])
    scores = mm(q, k, NT) * c
    expon = jnp.exp(scores - jnp.max(scores, axis=-1, keepdims=True))
    p = (expon * (1.0 / jnp.sum(expon, axis=-1, keepdims=True))).astype(BF)
    d_scores = (mm(dq, k, NT) + mm(q, dk, NT)) * c
    mixed = p.astype(F32) * d_scores
    row_sum = jnp.sum(mixed, axis=-1, keepdims=True)
    out = mm(mixed.astype(BF), v) + mm(p, dv) - row_sum * mm(p, v)
    probs[...] = p
    for i, value in enumerate((q, k, v)):
        primal[i] = value
    return out.astype(BF)


def near_kernel(gath, w_in, w_out, mods, tokens, term, primal, probs):
    blocks, _, rows, _ = gath.shape
    scale = 1.0 + mods[1:2, :]
    shift = mods[0:1, :]
    count = blocks * rows
    span = count // 2
    plain, changed = [], []
    for start in (0, span):
        for at in range(start, start + span, FEW):
            i, few = at // rows, pl.ds(at % rows, FEW)
            normed, inverse = normalize(gath[i, 0, few, :].astype(F32))
            tokens[pl.ds(at, FEW), :] = (normed * scale + shift).astype(BF)
            field = norm_tangent(gath[i, 1, few, :].astype(F32), normed, inverse)
            tokens[pl.ds(count + at, FEW), :] = (field * scale).astype(BF)
        plain.append(mm(tokens[pl.ds(start, span), :], w_in[...], NT))
        changed.append(mm(tokens[pl.ds(count + start, span), :], w_in[...], NT))
    projected = jnp.concatenate(plain + changed, axis=0)
    term[...] = mm(head_forward(projected, primal, probs), w_out[...])


def far_kernel(tokens, w_in, out, primal, probs):
    out[...] = head_forward(mm(tokens[...], w_in[...], NT), primal, probs)


def sum_kernel(term, out, w_out, parts):
    total = term[...] + mm(out[...], w_out[...])
    parts[...] = total.astype(BF).reshape(parts.shape)


def update_kernel(parts, probe, mods, gated, update):
    total = parts[0].astype(F32)
    for j in range(1, parts.shape[0]):
        total = total + parts[j].astype(F32)
    gate = mods[2:3, :]
    fresh = probe[0].astype(F32) + gate * total
    update[...] = fresh
    value = (gate * fresh).astype(BF)
    for j in range(gated.shape[0]):
        gated[j] = value


def adjoint_kernel(
    gated,
    near_in,
    near_out,
    near_primal,
    near_probs,
    far_in,
    far_out,
    far_primal,
    far_probs,
    parts,
    w_in,
):
    c = HEAD_DIM ** (-0.5)
    blocks, rows, width = gated.shape
    whole = gated[...].reshape(blocks * rows, width)
    third = 3 * HEAD_DIM
    w_in[pl.ds(0, third), :] = near_in[...].astype(F32)
    w_in[pl.ds(third, third), :] = far_in[...].astype(F32)
    grads = []
    for w_out, primal, probs in (
        (near_out, near_primal, near_probs),
        (far_out, far_primal, far_probs),
    ):
        co = mm(whole, w_out[...], NT).astype(BF)
        q, k, v = primal[0], primal[1], primal[2]
        p = probs[...]
        p_float = p.astype(F32)
        d_probs = mm(co, v, NT)
        row_dot = jnp.sum(p_float * d_probs, axis=-1, keepdims=True)
        scaled = (p_float * (d_probs - row_dot) * c).astype(BF)
        grads += [mm(scaled, k), mm(scaled, q, TN), mm(p, co, TN)]
    grads = jnp.concatenate(grads, axis=1).astype(BF)
    parts[...] = mm(grads, w_in[...].astype(BF)).astype(BF).reshape(parts.shape)


def pulled_kernel(parts, update, noisy, mods, pulled, lost):
    total = parts[0].astype(F32)
    for j in range(1, parts.shape[0]):
        total = total + parts[j].astype(F32)
    normed, inverse = normalize(noisy[...].astype(F32))
    value = update[...] + norm_tangent((1.0 + mods[1:2, :]) * total, normed, inverse)
    rounded = value.astype(BF)
    lost[...] = value - rounded.astype(F32)
    pairs, each, _ = pulled.shape
    for i in range(pairs):
        pulled[i] = value[i * each : (i + 1) * each].astype(BF)


def gram_kernel(scale, mine, other, copies, rows):
    first = lax.axis_index("core") == 0
    for i in range(mine.shape[0]):
        rows[2 * i] = jnp.where(first, mine[i], other[i])
        rows[2 * i + 1] = jnp.where(first, other[i], mine[i])
    each = [rows[:, t, :] for t in range(rows.shape[1])]
    gram = sum(mm(row, row, NT) for row in each) * scale
    n = gram.shape[0]
    width = LANES // n
    high = n // width
    packed = jnp.concatenate([gram[i * high : (i + 1) * high] for i in range(width)], axis=1)
    for j in range(copies.shape[0]):
        copies[j] = packed


def tree_sum(terms):
    while len(terms) > 1:
        terms = [terms[i] + terms[i + 1] for i in range(0, len(terms), 2)]
    return terms[0]


def total_kernel(arrived, copies):
    total = tree_sum([arrived[j] for j in range(arrived.shape[0])])
    for j in range(copies.shape[0]):
        copies[j] = total


def picked(n, core):
    row = lax.broadcasted_iota(jnp.int32, (n // 2, n), 0)
    col = lax.broadcasted_iota(jnp.int32, (n // 2, n), 1)
    return jnp.where(col == 2 * row + core, 1.0, 0.0)


def solve_kernel(arrived, rows, lost, factor, solved, rest):
    packed = tree_sum([arrived[j] for j in range(arrived.shape[0])])
    n = factor.shape[0]
    width = LANES // n
    a = jnp.concatenate([packed[:, i * n : (i + 1) * n] for i in range(width)], axis=0)
    both = jnp.concatenate([a, eye(n)], axis=1)
    row = lax.broadcasted_iota(jnp.int32, both.shape, 0)
    col = lax.broadcasted_iota(jnp.int32, both.shape, 1)
    wide = (1, both.shape[1])
    for j in range(0, n, STEP):
        span = range(STEP)
        tops = [both[j + i : j + i + 1, :] for i in span]
        sides = [jnp.broadcast_to(both[:, j + i : j + i + 1], both.shape) for i in span]
        corner = [
            [jnp.broadcast_to(tops[i][:, j + k : j + k + 1], wide) for k in span] for i in span
        ]
        change = jnp.zeros_like(both)
        for i in span:
            inverse = 1.0 / corner[i][i]
            for k in range(i + 1, STEP):
                ratio = corner[i][k] * inverse
                tops[k] = tops[k] - ratio * tops[i]
                sides[k] = sides[k] - ratio * sides[i]
                for m in range(k, STEP):
                    corner[k][m] = corner[k][m] - ratio * corner[i][m]
            change = change + sides[i] * (tops[i] * inverse)
        below = both - jnp.where(row >= j + STEP, change, 0.0)
        for i in span:
            below = jnp.where(row == j + i, tops[i], below)
        both = below
    pivots = jnp.sum(jnp.where(row == col, both, 0.0), axis=1, keepdims=True)
    both = both / jnp.sqrt(pivots)
    factor[...] = jnp.where(col >= row, both, 0.0)[:, :n]
    core = lax.axis_index("core")
    own = lax.axis_index("z") * 2 + core
    square = jnp.where((row == own) & (col == own), both, 0.0)
    pivot = jnp.sum(jnp.sum(square, axis=0, keepdims=True), axis=1, keepdims=True)
    rest[...] = lost[...] * (1.0 / pivot)
    remains = both[:, n:]
    choice = picked(n, core).astype(BF)
    pieces = []
    for _ in range(3):
        piece = remains.astype(BF)
        pieces.append(mm(choice, piece))
        remains = remains - piece.astype(F32)
    pieces = jnp.concatenate(pieces, axis=0).astype(BF)
    for t in range(rows.shape[1]):
        product = mm(pieces, rows[:, t, :])
        high, middle, low = [product[i * n // 2 : (i + 1) * n // 2] for i in range(3)]
        solved[:, t, :] = (high + (middle + low)).astype(BF)


def basis_kernel(pairs, rest, triangle, basis, factor):
    factor[...] = triangle[...]
    count, each, _ = pairs.shape
    for i in range(count):
        at = slice(i * each, (i + 1) * each)
        basis[0, at, :] = pairs[i].astype(F32) + rest[at, :]


HBM = pl.BlockSpec(memory_space=pl.ANY)
LOCAL = pl.BlockSpec(memory_space=pltpu.VMEM)


def call(
    kernel, out_shape, *args, where=None, out_specs=None, scratch=(), flops=0, moved=0, limit=8
):
    return pl.pallas_call(
        kernel,
        out_shape=out_shape,
        in_specs=where or [LOCAL] * len(args),
        out_specs=out_specs or jax.tree.map(lambda _: LOCAL, out_shape),
        scratch_shapes=list(scratch),
        compiler_params=pltpu.CompilerParams(vmem_limit_bytes=limit * MIB),
        cost_estimate=pl.CostEstimate(flops=flops, bytes_accessed=moved, transcendentals=0),
    )(*args)


def exchange(blocks, axis):
    return lax.all_to_all(blocks, axis, split_axis=0, concat_axis=0, tiled=True)


def shards(noisy, probes, w_qkv, w_out, w_mod, timestep):
    rows, width = noisy.shape
    parts, frames, cores, chips = [lax.axis_size(n) for n in ("part", "frame", "core", "z")]
    seq_count = parts * frames
    probe_count = cores * chips
    frame_rows = parts * rows

    outgoing = call(
        copies_kernel,
        jax.ShapeDtypeStruct((parts, 2, rows, width), BF),
        noisy,
        probes,
        where=[HBM, HBM],
        out_specs=HBM,
        scratch=(
            pltpu.VMEM((2, rows, width), BF),
            pltpu.SemaphoreType.DMA((2 + parts,)),
        ),
        moved=2 * 10**6,
        limit=60,
    )
    outgoing, w_in, w_out = lax.optimization_barrier((outgoing, w_qkv.T, w_out))
    gath = exchange(outgoing, "part")
    half = seq_count - seq_count // 4
    partner = [(i, i ^ half) for i in range(seq_count)]
    far_in = lax.ppermute(w_in, SEQ, partner)
    far_out = lax.ppermute(w_out, SEQ, partner)
    mods = modulation(timestep, w_mod, width)

    part_sums = jax.ShapeDtypeStruct((parts, rows, width), BF)
    kept = (
        jax.ShapeDtypeStruct((3, frame_rows, HEAD_DIM), BF),
        jax.ShapeDtypeStruct((frame_rows, frame_rows), BF),
    )
    tokens, term, near_primal, near_probs = call(
        near_kernel,
        (
            jax.ShapeDtypeStruct((2 * frame_rows, width), BF),
            jax.ShapeDtypeStruct((frame_rows, width), F32),
        )
        + kept,
        gath,
        w_in,
        w_out,
        mods,
        flops=10**9,
        moved=6 * 10**6,
        limit=24,
    )
    out, far_primal, far_probs = call(
        far_kernel,
        (jax.ShapeDtypeStruct((frame_rows, HEAD_DIM), BF),) + kept,
        tokens,
        far_in,
        flops=10**9,
        moved=4 * 10**6,
        limit=24,
    )
    sums = call(sum_kernel, part_sums, term, out, far_out, flops=10**8, moved=10**6)
    sums = exchange(sums, "part")
    gated, update = call(
        update_kernel,
        (part_sums, jax.ShapeDtypeStruct((rows, width), F32)),
        sums,
        probes,
        mods,
        moved=10**6,
    )
    gated = exchange(gated, "part")
    sums = call(
        adjoint_kernel,
        part_sums,
        gated,
        w_in,
        w_out,
        near_primal,
        near_probs,
        far_in,
        far_out,
        far_primal,
        far_probs,
        scratch=(pltpu.VMEM((6 * HEAD_DIM, width), F32),),
        flops=2 * 10**9,
        moved=5 * 10**6,
        limit=24,
    )
    sums = exchange(sums, "part")
    pairs = jax.ShapeDtypeStruct((chips, rows // chips, width), BF)
    own_rows = jax.ShapeDtypeStruct((rows, width), F32)
    pulled, lost = call(
        pulled_kernel, (pairs, own_rows), sums, update, noisy, mods, moved=10**6
    )
    mine = exchange(pulled, "z")
    other = lax.ppermute(mine, "core", [(i, i ^ 1) for i in range(cores)])
    high = probe_count * probe_count // LANES

    def blocks_of(count):
        return jax.ShapeDtypeStruct((count, high, LANES), F32)

    grams, every = call(
        functools.partial(gram_kernel, 1.0 / float(seq_count * rows * width)),
        (
            blocks_of(seq_count),
            jax.ShapeDtypeStruct((probe_count, rows // chips, width), BF),
        ),
        mine,
        other,
        moved=10**5,
    )
    grams = exchange(grams, SEQ)
    grams = call(total_kernel, blocks_of(chips), grams, moved=10**5)
    square = jax.ShapeDtypeStruct((probe_count, probe_count), F32)
    triangle, solved, rest = call(
        solve_kernel,
        (square, pairs, own_rows),
        exchange(grams, "z"),
        every,
        lost,
        moved=3 * 10**5,
    )
    basis, factor = call(
        basis_kernel,
        (jax.ShapeDtypeStruct((1, rows, width), F32), square),
        exchange(solved, "z"),
        rest,
        triangle,
        moved=3 * 10**5,
    )
    return basis, factor


def solution(mesh):
    split = Mesh(
        mesh.devices.reshape(
            mesh.shape["probe"] // 2, 2, FRAMES, mesh.shape["seq"] // FRAMES
        ),
        PROBE + SEQ,
    )
    placed = (P(SEQ, None), P(PROBE, SEQ, None), P(None, SEQ), P(SEQ, None), P(), P())
    return jax.shard_map(
        shards,
        mesh=split,
        in_specs=placed,
        out_specs=(P(PROBE, SEQ, None), P()),
        check_vma=False,
    )
```

```python
import functools
import math

import jax
import jax.numpy as jnp
from jax import lax
from jax.experimental import pallas as pl
from jax.experimental.pallas import tpu as pltpu
from jax.sharding import Mesh
from jax.sharding import PartitionSpec as P

HEAD_DIM = 72
LANES = 128
FRAMES = 2
SEQ = ("frame", "part")
PROBE = ("z", "core")
MIB = 1024 * 1024
STEP = 4
FEW = 16
NT = (((1,), (1,)), ((), ()))
NN = (((1,), (0,)), ((), ()))
TN = (((0,), (0,)), ((), ()))
BF = jnp.bfloat16
F32 = jnp.float32


def mm(a, b, dims=NN):
    return lax.dot_general(a, b, dims, preferred_element_type=F32)


def exact(a, b, dims=NN):
    return lax.dot_general(
        a, b, dims, precision=lax.Precision.HIGHEST, preferred_element_type=F32
    )


def eye(n):
    row = lax.broadcasted_iota(jnp.int32, (n, n), 0)
    col = lax.broadcasted_iota(jnp.int32, (n, n), 1)
    return jnp.where(row == col, 1.0, 0.0)


def modulation(timestep, w_mod, feat_width):
    half_dim = w_mod.shape[0] // 2
    freq_index = jnp.arange(half_dim, dtype=jnp.float32)
    frequency = jnp.exp(-math.log(10000.0) * freq_index / half_dim)
    angles = timestep[0].astype(jnp.float32) * frequency
    embedding = jnp.concatenate([jnp.cos(angles), jnp.sin(angles)])
    modulated = jnp.sum(jax.nn.silu(embedding)[:, None] * w_mod.astype(jnp.float32), axis=0)
    return modulated.reshape(3, feat_width)


def normalize(values_f):
    centered = values_f - jnp.mean(values_f, axis=-1, keepdims=True)
    inverse = 1.0 / jnp.sqrt(jnp.mean(centered * centered, axis=-1, keepdims=True) + 1e-06)
    return centered * inverse, inverse


def norm_tangent(field, normed, inverse):
    mean_part = jnp.mean(field, axis=-1, keepdims=True)
    along = jnp.mean(field * normed, axis=-1, keepdims=True)
    return (field - mean_part - normed * along) * inverse


def fetch(pairs, sems):
    copies = [pltpu.make_async_copy(a, b, sems.at[i]) for i, (a, b) in enumerate(pairs)]
    for copy in copies:
        copy.start()
    return copies


def copies_kernel(noisy, probe, out, staged, sems):
    count = out.shape[0]
    for copy in fetch([(noisy, staged.at[0]), (probe.at[0], staged.at[1])], sems):
        copy.wait()
    for copy in fetch([(staged, out.at[j]) for j in range(count)], sems.at[pl.ds(2, count)]):
        copy.wait()


def thirds(value):
    return [value[:, i * HEAD_DIM : (i + 1) * HEAD_DIM].astype(BF) for i in range(3)]


def head_forward(projected, primal, probs):
    c = HEAD_DIM ** (-0.5)
    count = projected.shape[0] // 2
    q, k, v = thirds(projected[:count])
    dq, dk, dv = thirds(projected[count:])
    scores = mm(q, k, NT) * c
    expon = jnp.exp(scores - jnp.max(scores, axis=-1, keepdims=True))
    p = (expon * (1.0 / jnp.sum(expon, axis=-1, keepdims=True))).astype(BF)
    beside = [jnp.concatenate(pair, axis=1) for pair in ((dq, q), (k, dk))]
    d_scores = mm(*beside, NT) * c
    mixed = p.astype(F32) * d_scores
    row_sum = jnp.sum(mixed, axis=-1, keepdims=True)
    out = mm(mixed.astype(BF), v) + mm(p, dv) - row_sum * mm(p, v)
    probs[...] = p
    for i, value in enumerate((q, k, v)):
        primal[i] = value
    return out.astype(BF)


def near_kernel(gath, w_in, w_out, mods, tokens, term, primal, probs):
    blocks, _, rows, _ = gath.shape
    scale = 1.0 + mods[1:2, :]
    shift = mods[0:1, :]
    count = blocks * rows
    span = count // 2
    plain, changed = [], []
    for start in (0, span):
        for at in range(start, start + span, FEW):
            i, few = at // rows, pl.ds(at % rows, FEW)
            normed, inverse = normalize(gath[i, 0, few, :].astype(F32))
            tokens[pl.ds(at, FEW), :] = (normed * scale + shift).astype(BF)
            field = norm_tangent(gath[i, 1, few, :].astype(F32), normed, inverse)
            tokens[pl.ds(count + at, FEW), :] = (field * scale).astype(BF)
        plain.append(mm(tokens[pl.ds(start, span), :], w_in[...], NT))
        changed.append(mm(tokens[pl.ds(count + start, span), :], w_in[...], NT))
    projected = jnp.concatenate(plain + changed, axis=0)
    term[...] = mm(head_forward(projected, primal, probs), w_out[...])


def far_kernel(tokens, w_in, out, primal, probs):
    out[...] = head_forward(mm(tokens[...], w_in[...], NT), primal, probs)


def sum_kernel(term, out, w_out, parts):
    total = term[...] + mm(out[...], w_out[...])
    parts[...] = total.astype(BF).reshape(parts.shape)


def update_kernel(parts, probe, mods, gated, update):
    total = parts[0].astype(F32)
    for j in range(1, parts.shape[0]):
        total = total + parts[j].astype(F32)
    gate = mods[2:3, :]
    fresh = probe[0].astype(F32) + gate * total
    update[...] = fresh
    value = (gate * fresh).astype(BF)
    for j in range(gated.shape[0]):
        gated[j] = value


def adjoint_kernel(
    gated,
    near_in,
    near_out,
    near_primal,
    near_probs,
    far_in,
    far_out,
    far_primal,
    far_probs,
    parts,
    w_in,
):
    c = HEAD_DIM ** (-0.5)
    blocks, rows, width = gated.shape
    whole = gated[...].reshape(blocks * rows, width)
    third = 3 * HEAD_DIM
    w_in[pl.ds(0, third), :] = near_in[...].astype(F32)
    w_in[pl.ds(third, third), :] = far_in[...].astype(F32)
    grads = []
    for w_out, primal, probs in (
        (near_out, near_primal, near_probs),
        (far_out, far_primal, far_probs),
    ):
        co = mm(whole, w_out[...], NT).astype(BF)
        q, k, v = primal[0], primal[1], primal[2]
        p = probs[...]
        p_float = p.astype(F32)
        d_probs = mm(co, v, NT)
        row_dot = jnp.sum(p_float * d_probs, axis=-1, keepdims=True)
        scaled = (p_float * (d_probs - row_dot) * c).astype(BF)
        grads += [mm(scaled, k), mm(scaled, q, TN), mm(p, co, TN)]
    grads = jnp.concatenate(grads, axis=1).astype(BF)
    parts[...] = mm(grads, w_in[...].astype(BF)).astype(BF).reshape(parts.shape)


def pulled_kernel(parts, update, noisy, mods, pulled, lost):
    total = parts[0].astype(F32)
    for j in range(1, parts.shape[0]):
        total = total + parts[j].astype(F32)
    normed, inverse = normalize(noisy[...].astype(F32))
    value = update[...] + norm_tangent((1.0 + mods[1:2, :]) * total, normed, inverse)
    rounded = value.astype(BF)
    lost[...] = value - rounded.astype(F32)
    pairs, each, _ = pulled.shape
    for i in range(pairs):
        pulled[i] = value[i * each : (i + 1) * each].astype(BF)


def gram_kernel(scale, mine, other, copies, rows):
    first = lax.axis_index("core") == 0
    for i in range(mine.shape[0]):
        rows[2 * i] = jnp.where(first, mine[i], other[i])
        rows[2 * i + 1] = jnp.where(first, other[i], mine[i])
    each = [rows[:, t, :] for t in range(rows.shape[1])]
    gram = sum(mm(row, row, NT) for row in each) * scale
    n = gram.shape[0]
    width = LANES // n
    high = n // width
    packed = jnp.concatenate([gram[i * high : (i + 1) * high] for i in range(width)], axis=1)
    for j in range(copies.shape[0]):
        copies[j] = packed


def tree_sum(terms):
    while len(terms) > 1:
        terms = [terms[i] + terms[i + 1] for i in range(0, len(terms), 2)]
    return terms[0]


def total_kernel(arrived, copies):
    total = tree_sum([arrived[j] for j in range(arrived.shape[0])])
    for j in range(copies.shape[0]):
        copies[j] = total


def picked(n, core):
    row = lax.broadcasted_iota(jnp.int32, (n // 2, n), 0)
    col = lax.broadcasted_iota(jnp.int32, (n // 2, n), 1)
    return jnp.where(col == 2 * row + core, 1.0, 0.0)


def solve_kernel(arrived, rows, lost, factor, solved, rest):
    packed = tree_sum([arrived[j] for j in range(arrived.shape[0])])
    n = factor.shape[0]
    width = LANES // n
    a = jnp.concatenate([packed[:, i * n : (i + 1) * n] for i in range(width)], axis=0)
    both = jnp.concatenate([a, eye(n)], axis=1)
    row = lax.broadcasted_iota(jnp.int32, both.shape, 0)
    col = lax.broadcasted_iota(jnp.int32, both.shape, 1)
    wide = (1, both.shape[1])
    for j in range(0, n, STEP):
        span = range(STEP)
        tops = [both[j + i : j + i + 1, :] for i in span]
        sides = [jnp.broadcast_to(both[:, j + i : j + i + 1], both.shape) for i in span]
        corner = [
            [jnp.broadcast_to(tops[i][:, j + k : j + k + 1], wide) for k in span] for i in span
        ]
        change = jnp.zeros_like(both)
        for i in span:
            inverse = 1.0 / corner[i][i]
            for k in range(i + 1, STEP):
                ratio = corner[i][k] * inverse
                tops[k] = tops[k] - ratio * tops[i]
                sides[k] = sides[k] - ratio * sides[i]
                for m in range(k, STEP):
                    corner[k][m] = corner[k][m] - ratio * corner[i][m]
            change = change + sides[i] * (tops[i] * inverse)
        below = both - jnp.where(row >= j + STEP, change, 0.0)
        for i in span:
            below = jnp.where(row == j + i, tops[i], below)
        both = below
    pivots = jnp.sum(jnp.where(row == col, both, 0.0), axis=1, keepdims=True)
    both = both / jnp.sqrt(pivots)
    factor[...] = jnp.where(col >= row, both, 0.0)[:, :n]
    core = lax.axis_index("core")
    own = lax.axis_index("z") * 2 + core
    square = jnp.where((row == own) & (col == own), both, 0.0)
    pivot = jnp.sum(jnp.sum(square, axis=0, keepdims=True), axis=1, keepdims=True)
    rest[...] = lost[...] * (1.0 / pivot)
    remains = both[:, n:]
    choice = picked(n, core).astype(BF)
    pieces = []
    for _ in range(3):
        piece = remains.astype(BF)
        pieces.append(mm(choice, piece))
        remains = remains - piece.astype(F32)
    pieces = jnp.concatenate(pieces, axis=0).astype(BF)
    for t in range(rows.shape[1]):
        product = mm(pieces, rows[:, t, :])
        high, middle, low = [product[i * n // 2 : (i + 1) * n // 2] for i in range(3)]
        solved[:, t, :] = (high + (middle + low)).astype(BF)


def basis_kernel(pairs, rest, triangle, basis, factor):
    factor[...] = triangle[...]
    count, each, _ = pairs.shape
    for i in range(count):
        at = slice(i * each, (i + 1) * each)
        basis[0, at, :] = pairs[i].astype(F32) + rest[at, :]


HBM = pl.BlockSpec(memory_space=pl.ANY)
LOCAL = pl.BlockSpec(memory_space=pltpu.VMEM)


def call(
    kernel, out_shape, *args, where=None, out_specs=None, scratch=(), flops=0, moved=0, limit=8
):
    return pl.pallas_call(
        kernel,
        out_shape=out_shape,
        in_specs=where or [LOCAL] * len(args),
        out_specs=out_specs or jax.tree.map(lambda _: LOCAL, out_shape),
        scratch_shapes=list(scratch),
        compiler_params=pltpu.CompilerParams(vmem_limit_bytes=limit * MIB),
        cost_estimate=pl.CostEstimate(flops=flops, bytes_accessed=moved, transcendentals=0),
    )(*args)


def exchange(blocks, axis):
    return lax.all_to_all(blocks, axis, split_axis=0, concat_axis=0, tiled=True)


def shards(noisy, probes, w_qkv, w_out, w_mod, timestep):
    rows, width = noisy.shape
    parts, frames, cores, chips = [lax.axis_size(n) for n in ("part", "frame", "core", "z")]
    seq_count = parts * frames
    probe_count = cores * chips
    frame_rows = parts * rows

    outgoing = call(
        copies_kernel,
        jax.ShapeDtypeStruct((parts, 2, rows, width), BF),
        noisy,
        probes,
        where=[HBM, HBM],
        out_specs=HBM,
        scratch=(
            pltpu.VMEM((2, rows, width), BF),
            pltpu.SemaphoreType.DMA((2 + parts,)),
        ),
        moved=2 * 10**6,
        limit=60,
    )
    outgoing, w_in, w_out = lax.optimization_barrier((outgoing, w_qkv.T, w_out))
    gath = exchange(outgoing, "part")
    half = seq_count - seq_count // 4
    partner = [(i, i ^ half) for i in range(seq_count)]
    far_in = lax.ppermute(w_in, SEQ, partner)
    far_out = lax.ppermute(w_out, SEQ, partner)
    mods = modulation(timestep, w_mod, width)

    part_sums = jax.ShapeDtypeStruct((parts, rows, width), BF)
    kept = (
        jax.ShapeDtypeStruct((3, frame_rows, HEAD_DIM), BF),
        jax.ShapeDtypeStruct((frame_rows, frame_rows), BF),
    )
    tokens, term, near_primal, near_probs = call(
        near_kernel,
        (
            jax.ShapeDtypeStruct((2 * frame_rows, width), BF),
            jax.ShapeDtypeStruct((frame_rows, width), F32),
        )
        + kept,
        gath,
        w_in,
        w_out,
        mods,
        flops=10**9,
        moved=6 * 10**6,
        limit=24,
    )
    out, far_primal, far_probs = call(
        far_kernel,
        (jax.ShapeDtypeStruct((frame_rows, HEAD_DIM), BF),) + kept,
        tokens,
        far_in,
        flops=10**9,
        moved=4 * 10**6,
        limit=24,
    )
    sums = call(sum_kernel, part_sums, term, out, far_out, flops=10**8, moved=10**6)
    sums = exchange(sums, "part")
    gated, update = call(
        update_kernel,
        (part_sums, jax.ShapeDtypeStruct((rows, width), F32)),
        sums,
        probes,
        mods,
        moved=10**6,
    )
    gated = exchange(gated, "part")
    sums = call(
        adjoint_kernel,
        part_sums,
        gated,
        w_in,
        w_out,
        near_primal,
        near_probs,
        far_in,
        far_out,
        far_primal,
        far_probs,
        scratch=(pltpu.VMEM((6 * HEAD_DIM, width), F32),),
        flops=2 * 10**9,
        moved=5 * 10**6,
        limit=24,
    )
    sums = exchange(sums, "part")
    pairs = jax.ShapeDtypeStruct((chips, rows // chips, width), BF)
    own_rows = jax.ShapeDtypeStruct((rows, width), F32)
    pulled, lost = call(
        pulled_kernel, (pairs, own_rows), sums, update, noisy, mods, moved=10**6
    )
    mine = exchange(pulled, "z")
    other = lax.ppermute(mine, "core", [(i, i ^ 1) for i in range(cores)])
    high = probe_count * probe_count // LANES

    def blocks_of(count):
        return jax.ShapeDtypeStruct((count, high, LANES), F32)

    grams, every = call(
        functools.partial(gram_kernel, 1.0 / float(seq_count * rows * width)),
        (
            blocks_of(seq_count),
            jax.ShapeDtypeStruct((probe_count, rows // chips, width), BF),
        ),
        mine,
        other,
        moved=10**5,
    )
    grams = exchange(grams, SEQ)
    grams = call(total_kernel, blocks_of(chips), grams, moved=10**5)
    square = jax.ShapeDtypeStruct((probe_count, probe_count), F32)
    triangle, solved, rest = call(
        solve_kernel,
        (square, pairs, own_rows),
        exchange(grams, "z"),
        every,
        lost,
        moved=3 * 10**5,
    )
    basis, factor = call(
        basis_kernel,
        (jax.ShapeDtypeStruct((1, rows, width), F32), square),
        exchange(solved, "z"),
        rest,
        triangle,
        moved=3 * 10**5,
    )
    return basis, factor


def solution(mesh):
    split = Mesh(
        mesh.devices.reshape(
            mesh.shape["probe"] // 2, 2, FRAMES, mesh.shape["seq"] // FRAMES
        ),
        PROBE + SEQ,
    )
    placed = (P(SEQ, None), P(PROBE, SEQ, None), P(None, SEQ), P(SEQ, None), P(), P())
    return jax.shard_map(
        shards,
        mesh=split,
        in_specs=placed,
        out_specs=(P(PROBE, SEQ, None), P()),
        check_vma=False,
    )
```
